512 devices in a mesh: section: 4 (over y_hi, core), lat: 8 (over x, y_lo), lon: 16 (over z).
Axes of the slice: x: 4, y: 4 (y_hi: 2, y_lo: 2; y = y_hi * 2 + y_lo), z: 16, core: 2. Of those that a mesh axis runs over, the one named last changes fastest.
Arguments:
- block_inputs: bfloat16 [4, 2, 48, 192, 384], P('section', None, 'lat', 'lon'), may hold values from -6 to 6
- cotangent: bfloat16 [2, 48, 192, 384], P(None, 'lat', 'lon'), may hold values from -6 to 6
- input_projection: bfloat16 [4, 384, 1152], P('section'), may hold values from -0.3125 to 0.3125
- output_projection: bfloat16 [4, 384, 384], P('section'), may hold values from -0.3125 to 0.3125
- norm_gain: float32 [4, 384], P('section'), may hold values from 0.5 to 1.5
- earth_bias: float32 [4, 1, 8, 12, 3312], P('section', None, 'lat'), may hold values from -6 to 6
Outputs:
- input_grads: bfloat16 [4, 2, 48, 192, 384], P('section', None, 'lat', 'lon')
- entry_grads: float32 [4, 384, 1152], P('section', None, ('lat', 'lon'))
- exit_grads: float32 [4, 384, 384], P('section', None, ('lat', 'lon'))
- gain_grads: float32 [4, 384], P('section', ('lat', 'lon'))
- bias_grads: float32 [4, 1, 8, 12, 3312], P('section', None, 'lat', None, 'lon')
The draws below stay inside these ranges and needn't reach their ends.
All inputs are finite; a program needn't handle non-finite values.
Results may differ from the reference program's by a relative error of at most 0.035.
Values may be sent and summed in bfloat16 or wider, within the bound.
A program may use at most 128 MiB of HBM per device.

```python
import jax
import jax.numpy as jnp
from jax import lax

C = 384
HEADS = 12
HEAD_DIM = 32
WZ = 2
WLAT = 6
WLON = 12
LEVELS = 2
WIN = 144
ZW = 1
NLATW = 8
NLAT = 48
NLONW = 16
NLON = 192
RELPOS = 3312
LAYERS = 4


def level_of(stream_key, dims, cuts, low, largest):
    def one(dim, blocks):
        steps = jax.random.uniform(jax.random.fold_in(jax.random.fold_in(stream_key, 6), dim), (blocks,), jnp.float32, low / len(cuts), largest / len(cuts))
        return jnp.repeat(jnp.exp(steps), dims[dim] // blocks).reshape((-1,) + (1,) * (len(dims) - dim - 1))

    loudness = one(*cuts[0])
    for cut in cuts[1:]:
        loudness = loudness * one(*cut)
    return loudness


def scatter_about(own_key, extent, scale, limit, cuts=(), held_as=jnp.bfloat16):
    values = jax.random.normal(own_key, extent, jnp.float32) * scale
    if len(cuts) > 0:
        values = level_of(own_key, extent, cuts, -0.22, 0.18) * values
    return jnp.clip(values, min=-limit, max=limit).astype(held_as)


def setup_inputs(seed: int = 0) -> dict:
    splits = jax.random.split(jax.random.key(seed), 7)
    block_inputs = scatter_about(splits[0], (LAYERS, LEVELS, NLAT, NLON, C), 1.0, 6.0, ((0, 4), (2, 8), (3, 16)))
    cotangent = scatter_about(splits[1], (LEVELS, NLAT, NLON, C), 1.0, 6.0, ((1, 8), (2, 16)))
    input_projection = scatter_about(splits[2], (LAYERS, C, 3 * C), C ** -0.5, 0.3125, ((0, 4),))
    output_projection = scatter_about(splits[3], (LAYERS, C, C), C ** -0.5, 0.3125, ((0, 4),))
    norm_gain = jnp.clip(1.0 + 0.1 * jax.random.normal(splits[4], (LAYERS, C), jnp.float32), 0.5, 1.5)
    earth_bias = scatter_about(splits[5], (LAYERS, ZW, NLATW, HEADS, RELPOS), 1.0, 6.0, ((0, 4), (2, 8)), jnp.float32)
    return dict(block_inputs=block_inputs, cotangent=cotangent, input_projection=input_projection, output_projection=output_projection, norm_gain=norm_gain, earth_bias=earth_bias)


EPS = 1e-05
HIGH = lax.Precision.HIGHEST

def pair_table():
    offsets = jnp.arange(2 * WLON - 1, dtype=jnp.int32)[:, None]
    query_col = jnp.arange(WLON, dtype=jnp.int32)[:, None]
    key_col = jnp.arange(WLON, dtype=jnp.int32)[None, :]
    pairs = (query_col - key_col + WLON - 1).reshape(1, WLON * WLON)
    return (offsets == pairs).astype(jnp.float32)

def expand_bias(table):
    groups = table.shape[0]
    split = table.reshape(groups, HEADS, WZ, WZ, WLAT, WLAT, 2 * WLON - 1)
    spread = jnp.einsum('ghzyabd,dm->ghzyabm', split, pair_table(), precision=HIGH)
    spread = spread.reshape(groups, HEADS, WZ, WZ, WLAT, WLAT, WLON, WLON)
    spread = spread.transpose(0, 1, 2, 4, 6, 3, 5, 7)
    return spread.reshape(groups, HEADS, WIN, WIN)

def fold_bias(grads):
    groups = grads.shape[0]
    parts = grads.reshape(groups, HEADS, WZ, WLAT, WLON, WZ, WLAT, WLON).transpose(0, 1, 2, 5, 3, 6, 4, 7)
    parts = parts.reshape(groups, HEADS, WZ, WZ, WLAT, WLAT, WLON * WLON)
    folded = jnp.einsum('ghzyabm,dm->ghzyabd', parts, pair_table(), precision=HIGH)
    return folded.reshape(groups, HEADS, RELPOS)

def window_regions(lat_window, lat_windows):
    levels = jnp.arange(LEVELS, dtype=jnp.int32).reshape(ZW, WZ)
    level_region = jnp.where(levels < LEVELS - WZ, 0, jnp.where(levels < LEVELS - WZ // 2, 1, 2))
    rows = jnp.arange(WLAT, dtype=jnp.int32)
    row_region = jnp.where(lat_window == lat_windows - 1, jnp.where(rows < WLAT - WLAT // 2, 1, 2), 0)
    region = level_region[:, :, None, None] * 3 + row_region[None, None, :, None] + jnp.zeros((1, 1, 1, WLON), jnp.int32)
    region = region.reshape(ZW, WIN)
    return region[:, :, None] == region[:, None, :]

def attention_backward(shifted, grad_out, entry_weight, exit_weight, bias, allowed):
    zcount, lcount = (shifted.shape[0], shifted.shape[1])
    flat = shifted.reshape(-1, C)
    projected = jnp.dot(flat, entry_weight, preferred_element_type=jnp.float32).astype(jnp.bfloat16)
    projected = lax.optimization_barrier(projected).astype(jnp.float32)
    projected = projected.reshape(zcount, lcount, WIN, 3, HEADS, HEAD_DIM)
    queries = projected[:, :, :, 0]
    keys = projected[:, :, :, 1]
    values = projected[:, :, :, 2]
    scale = HEAD_DIM ** (-0.5)
    scores = jnp.einsum('zlqhd,zlkhd->zlhqk', queries, keys, precision=HIGH) * scale + bias[:, None]
    raised = jnp.where(allowed[:, None, None], jnp.exp(scores), 0.0)
    attention = raised / lax.optimization_barrier(jnp.sum(raised, axis=-1, keepdims=True))
    attention_low = lax.optimization_barrier(attention.astype(jnp.bfloat16)).astype(jnp.float32)
    mixed = jnp.einsum('zlhqk,zlkhd->zlqhd', attention_low, values, precision=HIGH).astype(jnp.bfloat16).reshape(-1, C)
    grad_flat = grad_out.reshape(-1, C)
    exit_grad = jnp.dot(mixed.T, grad_flat, preferred_element_type=jnp.float32)
    mixed_grad = jnp.dot(grad_flat, exit_weight.T, preferred_element_type=jnp.float32).astype(jnp.bfloat16)
    mixed_grad = lax.optimization_barrier(mixed_grad).astype(jnp.float32).reshape(zcount, lcount, WIN, HEADS, HEAD_DIM)
    attention_grad = jnp.einsum('zlqhd,zlkhd->zlhqk', mixed_grad, values, precision=HIGH)
    value_grad = jnp.einsum('zlhqk,zlqhd->zlkhd', attention_low, mixed_grad, precision=HIGH)
    score_grad = attention * (attention_grad - lax.optimization_barrier(jnp.sum(attention_grad * attention, axis=-1, keepdims=True)))
    score_low = lax.optimization_barrier(score_grad.astype(jnp.bfloat16)).astype(jnp.float32)
    query_grad = jnp.einsum('zlhqk,zlkhd->zlqhd', score_low, keys, precision=HIGH) * scale
    key_grad = jnp.einsum('zlhqk,zlqhd->zlkhd', score_low, queries, precision=HIGH) * scale
    projected_grad = jnp.stack([query_grad, key_grad, value_grad], axis=3).astype(jnp.bfloat16).reshape(-1, 3 * C)
    entry_grad = jnp.dot(flat.T, projected_grad, preferred_element_type=jnp.float32)
    shifted_grad = jnp.dot(projected_grad, entry_weight.T, preferred_element_type=jnp.float32).astype(jnp.bfloat16)
    return (shifted_grad.reshape(shifted.shape), entry_grad, exit_grad, score_grad)

def to_windows(tile):
    split = tile.reshape(ZW, WZ, NLATW, WLAT, NLONW, WLON, C).transpose(2, 0, 4, 1, 3, 5, 6)
    return split.reshape(NLATW, ZW, NLONW, WIN, C)

def layer_backward(inputs, grad, entry_weight, exit_weight, gain_row, table):
    values_in = inputs.astype(jnp.float32)
    mean_row = lax.optimization_barrier(jnp.mean(values_in, axis=-1, keepdims=True))
    centered = values_in - mean_row
    inverse_std = lax.rsqrt(lax.optimization_barrier(jnp.mean(centered * centered, axis=-1, keepdims=True)) + EPS)
    normed = centered * inverse_std
    hidden = (normed * gain_row).astype(jnp.bfloat16)
    offsets = (-(WZ // 2), -(WLAT // 2), -(WLON // 2))
    shifted = jnp.roll(hidden, offsets, (0, 1, 2))
    grad_shifted = jnp.roll(grad, offsets, (0, 1, 2))

    def per_window(item):
        lat_window, shifted_rows, grad_rows, table_rows = item
        bias = expand_bias(table_rows)
        allowed = window_regions(lat_window, NLATW)
        shifted_grad, entry_grad, exit_grad, score_grad = attention_backward(shifted_rows, grad_rows, entry_weight, exit_weight, bias, allowed)
        return (shifted_grad, entry_grad, exit_grad, fold_bias(lax.optimization_barrier(jnp.sum(score_grad, axis=1))))
    shifted_grad, entry_parts, exit_parts, bias_parts = lax.map(per_window, (jnp.arange(NLATW, dtype=jnp.int32), to_windows(shifted), to_windows(grad_shifted), table.transpose(1, 0, 2, 3)))
    grid_grad = shifted_grad.reshape(NLATW, ZW, NLONW, WZ, WLAT, WLON, C).transpose(1, 3, 0, 4, 2, 5, 6)
    grid_grad = grid_grad.reshape(LEVELS, NLAT, NLON, C)
    rolled = jnp.roll(grid_grad, (WZ // 2, WLAT // 2, WLON // 2), (0, 1, 2))
    hidden_grad = lax.optimization_barrier(rolled).astype(jnp.float32)
    gain_grad = lax.optimization_barrier(jnp.sum(hidden_grad * normed, axis=(0, 1, 2)))
    normed_grad = hidden_grad * gain_row
    inner = normed_grad - lax.optimization_barrier(jnp.mean(normed_grad, axis=-1, keepdims=True)) - normed * lax.optimization_barrier(jnp.mean(normed_grad * normed, axis=-1, keepdims=True))
    input_grad = (grad.astype(jnp.float32) + inverse_std * inner).astype(jnp.bfloat16)
    return (input_grad, lax.optimization_barrier(jnp.sum(entry_parts, axis=0)), lax.optimization_barrier(jnp.sum(exit_parts, axis=0)), gain_grad, bias_parts.transpose(1, 0, 2, 3))

def stacked(results, slot):
    return jnp.stack([entry[slot] for entry in results])

def reference(block_inputs, cotangent, input_projection, output_projection, norm_gain, earth_bias):
    grad = cotangent
    results = [None] * LAYERS
    for layer in range(LAYERS - 1, -1, -1):
        results[layer] = layer_backward(block_inputs[layer], grad, input_projection[layer], output_projection[layer], norm_gain[layer], earth_bias[layer])
        grad = results[layer][0]
    return (stacked(results, 0), stacked(results, 1), stacked(results, 2), stacked(results, 3), stacked(results, 4))
```

```python
import functools

import jax
import jax.numpy as jnp
import numpy as np
from jax import lax
from jax.experimental import pallas as pl
from jax.experimental.pallas import tpu as pltpu
from jax.sharding import PartitionSpec as P

MESH = pl.DeviceIdType.MESH
F32 = jnp.float32
BF16 = jnp.bfloat16

C = 384
HEADS = 12
HEAD_DIM = 32
WLAT = 6
WLON = 12
LEVELS = 2
TOK = WLAT * WLON
WIN = LEVELS * TOK
SPAN = 2 * WLON - 1
RELPOS = 3312
LANES = 128
GROUPS = C // LANES
PER_GROUP = LANES // HEAD_DIM
STACK = PER_GROUP * TOK
ROWS = LEVELS * HEADS * TOK
PAIRS = LEVELS * HEADS * WLAT
EPS = 1e-05
SCALE = HEAD_DIM ** -0.5
OFF = -1e30
BIAS_ROWS = (0, 1, 3, 4)


def round_up(n, m):
    return (n + m - 1) // m * m


def spread_table():
    out = np.zeros((2 * LANES, WLON, LANES), np.float32)
    for lq in range(WLON):
        for ak in range(WLAT):
            for lk in range(WLON):
                out[ak * SPAN + lq - lk + WLON - 1, lq, ak * WLON + lk] = 1.0
    return out.reshape(2 * LANES, WLON * LANES)


def share_table(entry, exits, gains, parts, rows):
    out = np.zeros((parts, rows, entry + exits + gains), np.float32)
    e, x = entry // parts, exits // parts
    for j in range(parts):
        for r in range(e):
            out[j, r, j * e + r] = 1.0
        for r in range(x):
            out[j, e + r, entry + j * x + r] = 1.0
        out[j, e + x, entry + exits] = 1.0
    return out.reshape(parts * rows, -1)


def dot(a, b):
    return jnp.dot(a, b, preferred_element_type=F32)


def dot_t(a, b):
    return lax.dot_general(a, b, (((1,), (1,)), ((), ())), preferred_element_type=F32)


def t_dot(a, b):
    return lax.dot_general(a, b, (((0,), (0,)), ((), ())), preferred_element_type=F32)


def kernel(
    sizes, names,
    x_hbm, ct_hbm, wi_hbm, wo_hbm, gain_hbm, tab_hbm, s_hbm, p2_hbm,
    ig_out, red_out, bias_out,
    xin, cin, wi_v, wo_v, gain_v, tab_v, s_v, p2_v, t0, t1, bias, xs, gs, att, qm, kp, vp, mix, ds, pg,
    gsend, grecv, rb, rbr, sb1, rb1, sb2, rb2, bsb, brb,
    load_sem, xsend_sem, xrecv_sem, csend_sem, crecv_sem, gsend_sem, grecv_sem, bksend_sem, bkrecv_sem,
    s1send, s1recv, s2send, s2recv, bsend_sem, brecv_sem,
):
    ns, na, no = sizes
    sec, lat, lon = (lax.axis_index(name) for name in names)
    n_sec, n_lat, n_lon = names

    def at_lat(k):
        return lax.rem(lat + k + na, na)

    def at_lon(k):
        return lax.rem(lon + k + no, no)

    first, last = sec == 0, sec == ns - 1

    barrier = pltpu.get_barrier_semaphore()
    greeted = [{n_lat: at_lat(k)} for k in range(1, na)] + [{n_lon: at_lon(k)} for k in range(1, no)]
    greeted += [{n_lat: at_lat(k), n_lon: at_lon(k)} for k in (-1, 1)]
    for device in greeted:
        pl.semaphore_signal(barrier, inc=1, device_id=device, device_id_type=MESH)

    @pl.when(jnp.logical_not(first))
    def _():
        pl.semaphore_signal(barrier, inc=1, device_id={n_sec: sec - 1}, device_id_type=MESH)

    @pl.when(jnp.logical_not(last))
    def _():
        pl.semaphore_signal(barrier, inc=1, device_id={n_sec: sec + 1}, device_id_type=MESH)

    loads = [
        (tab_hbm.at[0, 0, 0], tab_v), (s_hbm, s_v), (x_hbm.at[0, :, pl.ds(3, 3)], xin.at[0]), (gain_hbm, gain_v),
        (wi_hbm.at[0], wi_v), (wo_hbm.at[0], wo_v), (p2_hbm, p2_v), (ct_hbm.at[:, pl.ds(3, 3)], cin.at[0]),
    ]
    loads = [pltpu.make_async_copy(src, dst, load_sem.at[i]) for i, (src, dst) in enumerate(loads)]
    for copy in loads:
        copy.start()

    pl.semaphore_wait(barrier, len(greeted) + jnp.minimum(sec, 1) + jnp.minimum(ns - 1 - sec, 1))

    def roll_copies(src, buffers, send, recv):
        plan = (
            ({n_lon: at_lon(-1)}, 3), ({n_lat: at_lat(-1)}, 0), ({n_lat: at_lat(-1), n_lon: at_lon(-1)}, 0),
        )
        return [
            pltpu.make_async_remote_copy(
                src_ref=src.at[:, pl.ds(row, 3)], dst_ref=buffers.at[i + 1], send_sem=send.at[i], recv_sem=recv.at[i],
                device_id=device, device_id_type=MESH,
            )
            for i, (device, row) in enumerate(plan)
        ]

    x_copies = roll_copies(x_hbm.at[0], xin, xsend_sem, xrecv_sem)
    for copy in x_copies:
        copy.start()
    c_copies = roll_copies(ct_hbm, cin, csend_sem, crecv_sem)

    @pl.when(last)
    def _():
        for copy in c_copies:
            copy.start()

    def assemble(buffers, out):
        for z in range(LEVELS):
            for a in range(WLAT):
                left, right = (0, 1) if a < 3 else (2, 3)
                row = z * TOK + a * WLON
                out[row:row + 6, :] = buffers[left, 1 - z, a % 3].astype(F32)[6:12]
                out[row + 6:row + 12, :] = buffers[right, 1 - z, a % 3].astype(F32)[0:6]

    loads[0].wait()
    loads[1].wait()
    width = WLAT * SPAN
    for z in range(LEVELS):
        for a in range(WLAT):
            start = (z * 3 * WLAT + a) * width
            rows = pl.ds(z * HEADS * WLAT + a, HEADS, stride=WLAT)
            t0[rows, :] = tab_v[:, start:start + LANES]
            rest = tab_v[:, start + LANES:start + width]
            t1[rows, :] = jnp.concatenate([rest, jnp.zeros((HEADS, 2 * LANES - width), F32)], axis=1)
    table = jnp.concatenate([t0[...], t1[...]], axis=1)
    table_high = table.astype(BF16)
    table_low = (table - table_high.astype(F32)).astype(BF16)
    query_row = lax.rem(lax.broadcasted_iota(jnp.int32, (PAIRS, LANES), 0), WLAT)
    key = lax.broadcasted_iota(jnp.int32, (PAIRS, LANES), 1)
    apart = jnp.logical_and((query_row < 3) != (key < TOK // 2), lat == na - 1)
    closed = jnp.where(jnp.logical_or(apart, key >= TOK), OFF, 0.0)
    closed = jnp.concatenate([closed, closed], axis=1)
    for i in range(WLON // 2):
        spread = s_v[:, 2 * i * LANES:(2 * i + 2) * LANES]
        part = dot(table_high, spread) + dot(table_low, spread) + closed
        bias[pl.ds(2 * i, PAIRS, stride=WLON), :] = part[:, :LANES]
        bias[pl.ds(2 * i + 1, PAIRS, stride=WLON), :] = part[:, LANES:]

    loads[2].wait()
    for copy in x_copies:
        copy.wait_recv()
    assemble(xin, xs)
    x = xs[...]
    centered = x - jnp.mean(x, axis=-1, keepdims=True)
    inverse = lax.rsqrt(jnp.mean(centered * centered, axis=-1, keepdims=True) + EPS)
    normed = centered * inverse
    loads[3].wait()
    gain = gain_v[...]
    hidden = (normed * gain).astype(BF16)
    loads[4].wait()
    projected = dot(hidden, wi_v[...]).astype(BF16).astype(F32)

    head_of_lane = lax.broadcasted_iota(jnp.int32, (TOK, LANES), 1) // HEAD_DIM

    def stack_heads(part):
        return jnp.concatenate([jnp.where(head_of_lane == h, part, 0.0) for h in range(PER_GROUP)], axis=0).astype(BF16)

    def unstack_heads(stacked):
        total = jnp.where(head_of_lane == 0, stacked[0:TOK], 0.0)
        for h in range(1, PER_GROUP):
            total = jnp.where(head_of_lane == h, stacked[h * TOK:(h + 1) * TOK], total)
        return total

    def pad_keys(part):
        return jnp.concatenate([part, jnp.zeros((LANES - TOK, LANES), F32)], axis=0).astype(BF16)

    places = [(z, g) for z in range(LEVELS) for g in range(GROUPS)]
    for i, (z, g) in enumerate(places):
        tokens, lanes = slice(z * TOK, (z + 1) * TOK), slice(g * LANES, (g + 1) * LANES)
        stacked_rows = slice(i * STACK, (i + 1) * STACK)
        queries = stack_heads(projected[tokens, g * LANES:(g + 1) * LANES])
        keys = pad_keys(projected[tokens, C + g * LANES:C + (g + 1) * LANES])
        values = pad_keys(projected[tokens, 2 * C + g * LANES:2 * C + (g + 1) * LANES])
        qm[i] = queries
        kp[i] = keys
        vp[i] = values
        raised = jnp.exp(dot_t(queries, keys) * SCALE + bias[stacked_rows, :])
        attention = raised / jnp.sum(raised, axis=-1, keepdims=True)
        att[stacked_rows, :] = attention
        mix[tokens, lanes] = unstack_heads(dot(attention.astype(BF16), values))

    loads[7].wait()

    @pl.when(last)
    def _():
        for copy in c_copies:
            copy.wait_recv()
        assemble(cin, gs)

    down = pltpu.make_async_remote_copy(
        src_ref=gsend, dst_ref=grecv, send_sem=gsend_sem, recv_sem=grecv_sem,
        device_id={n_sec: jnp.maximum(sec - 1, 0)}, device_id_type=MESH,
    )

    @pl.when(jnp.logical_not(last))
    def _():
        down.wait_recv()
        gs[...] = grecv[...].astype(F32)

    grad = gs[...]
    grad_low = grad.astype(BF16)
    loads[5].wait()
    mixed_grad = dot_t(grad_low, wo_v[...]).astype(BF16).astype(F32)
    for i, (z, g) in enumerate(places):
        tokens, lanes = slice(z * TOK, (z + 1) * TOK), slice(g * LANES, (g + 1) * LANES)
        stacked_rows = slice(i * STACK, (i + 1) * STACK)
        outer = stack_heads(mixed_grad[tokens, lanes])
        attention = att[stacked_rows, :]
        attention_grad = dot_t(outer, vp[i])
        score = attention * (attention_grad - jnp.sum(attention_grad * attention, axis=-1, keepdims=True))
        ds[stacked_rows, :] = score
        score_low = score.astype(BF16)
        pg[tokens, g * LANES:(g + 1) * LANES] = unstack_heads(dot(score_low, kp[i])) * SCALE
        pg[tokens, C + g * LANES:C + (g + 1) * LANES] = t_dot(score_low, qm[i])[:TOK] * SCALE
        pg[tokens, 2 * C + g * LANES:2 * C + (g + 1) * LANES] = t_dot(attention.astype(BF16), outer)[:TOK]

    projected_grad = pg[...].astype(BF16)
    hidden_grad = dot_t(projected_grad, wi_v[...]).astype(BF16).astype(F32)
    normed_grad = hidden_grad * gain
    along = jnp.mean(normed_grad * normed, axis=-1, keepdims=True)
    inner = normed_grad - jnp.mean(normed_grad, axis=-1, keepdims=True) - normed * along
    input_grad = grad + inverse * inner
    gsend[...] = input_grad.astype(BF16)

    @pl.when(jnp.logical_not(first))
    def _():
        down.start()

    for z in range(LEVELS):
        for a in range(WLAT):
            row = z * TOK + a * WLON
            rb[1 - z, a] = input_grad[row:row + WLON].astype(BF16)
    plan = (
        ({n_lon: at_lon(1)}, 0), ({n_lat: at_lat(1)}, 3), ({n_lat: at_lat(1), n_lon: at_lon(1)}, 3),
    )
    back_copies = [
        pltpu.make_async_remote_copy(
            src_ref=rb.at[:, pl.ds(row, 3)], dst_ref=rbr.at[i], send_sem=bksend_sem.at[i], recv_sem=bkrecv_sem.at[i],
            device_id=device, device_id_type=MESH,
        )
        for i, (device, row) in enumerate(plan)
    ]
    for copy in back_copies:
        copy.start()

    e1, x1 = 3 * C // na, C // na
    entry = t_dot(projected_grad, hidden)
    exits = t_dot(grad_low, mix[...].astype(BF16))
    gain_grad = jnp.sum(hidden_grad * normed, axis=0, keepdims=True)
    gain_rows = jnp.concatenate([gain_grad, jnp.zeros((15, C), F32)], axis=0).astype(BF16)
    for i in range(na):
        sb1[i, 0:e1] = entry[i * e1:(i + 1) * e1].astype(BF16)
        sb1[i, e1:e1 + x1] = exits[i * x1:(i + 1) * x1].astype(BF16)
        sb1[i, e1 + x1:e1 + x1 + 16] = gain_rows
    first_copies = [
        pltpu.make_async_remote_copy(
            src_ref=sb1.at[at_lat(k)], dst_ref=rb1.at[k], send_sem=s1send.at[k], recv_sem=s1recv.at[k],
            device_id={n_lat: at_lat(k)}, device_id_type=MESH,
        )
        for k in range(1, na)
    ]
    for copy in first_copies:
        copy.start()

    folded = jnp.zeros((PAIRS, 2 * LANES), F32)
    for lq in range(WLON):
        part = ds[pl.ds(lq, PAIRS, stride=WLON), :].astype(BF16)
        folded += dot_t(part, s_v[:, lq * LANES:(lq + 1) * LANES])
    t0[...] = folded[:, :LANES]
    t1[...] = folded[:, LANES:]
    quiet = jnp.zeros((16 - HEADS, 2 * LANES), F32)
    for u in range(8):
        parts = []
        for a in (BIAS_ROWS[u % 4], BIAS_ROWS[u % 4] + 1):
            rows = pl.ds(u // 4 * HEADS * WLAT + a, HEADS, stride=WLAT)
            parts += [jnp.concatenate([t0[rows, :], t1[rows, :]], axis=1), quiet]
        bsb[u] = jnp.concatenate(parts, axis=0).astype(BF16)
    if no == 16:
        def bias_copy(u, k):
            target = u if u < 4 else u + 8
            return target, pltpu.make_async_remote_copy(
                src_ref=bsb.at[u], dst_ref=brb.at[k], send_sem=bsend_sem.at[u], recv_sem=brecv_sem.at[k],
                device_id={n_lon: jnp.int32(target)}, device_id_type=MESH,
            )

        for u in range(8):
            target, copy = bias_copy(u, lon)

            @pl.when(lon != target)
            def _(copy=copy):
                copy.start()

    for copy in first_copies:
        copy.wait_recv()
    total = sb1[lat].astype(F32)
    for k in range(1, na):
        total += rb1[k].astype(F32)
    r2 = sb2.shape[1]
    loads[6].wait()
    sb2[...] = dot(p2_v[...], total.astype(BF16)).astype(BF16).reshape(no, r2, C)
    second_copies = [
        pltpu.make_async_remote_copy(
            src_ref=sb2.at[at_lon(k)], dst_ref=rb2.at[k], send_sem=s2send.at[k], recv_sem=s2recv.at[k],
            device_id={n_lon: at_lon(k)}, device_id_type=MESH,
        )
        for k in range(1, no)
    ]
    for copy in second_copies:
        copy.start()

    for copy in back_copies:
        copy.wait_recv()
    for z in range(LEVELS):
        for r in range(WLAT):
            if r >= 3:
                left, right = rbr[0, z, r - 3], rb[z, r - 3]
            else:
                left, right = rbr[2, z, r], rbr[1, z, r]
            ig_out[z, r] = jnp.concatenate([left.astype(F32)[6:12], right.astype(F32)[0:6]], axis=0).astype(BF16)

    if no == 16:
        keeps = jnp.logical_or(lon < 4, lon >= 12)
        bias_out[...] = jnp.zeros_like(bias_out)

        @pl.when(keeps)
        def _():
            for s in range(no):
                @pl.when(lon != s)
                def _():
                    bias_copy(0, s)[1].wait_recv()
            mine = jnp.where(lon < 4, lon, lon - 8)
            brb[lon] = bsb[mine]
            bias_total = brb[0].astype(F32)
            for s in range(1, no):
                bias_total += brb[s].astype(F32)
            bias_out[...] = bias_total

        for u in range(8):
            target, copy = bias_copy(u, lon)

            @pl.when(lon != target)
            def _(copy=copy):
                copy.wait_send()
    else:
        bias_out[...] = jnp.zeros_like(bias_out)

    for copy in second_copies:
        copy.wait_recv()
    total = sb2[lon].astype(F32)
    for k in range(1, no):
        total += rb2[k].astype(F32)
    red_out[...] = total

    for copy in x_copies + back_copies + first_copies + second_copies:
        copy.wait_send()

    @pl.when(last)
    def _():
        for copy in c_copies:
            copy.wait_send()

    @pl.when(jnp.logical_not(first))
    def _():
        down.wait_send()


def call_kernel(sizes, names, args):
    ns, na, no = sizes
    e1, x1 = 3 * C // na, C // na
    r1 = e1 + x1 + 16
    e2, x2 = e1 // no, x1 // no
    r2 = round_up(e2 + x2 + 1, 16)
    spread = jnp.asarray(spread_table(), BF16)
    shares = jnp.asarray(share_table(e1, x1, 16, no, r2), BF16)
    anywhere = pl.BlockSpec(memory_space=pl.ANY)
    vmem = pl.BlockSpec(memory_space=pltpu.VMEM)
    dma = pltpu.SemaphoreType.DMA
    n = LEVELS * GROUPS
    return pl.pallas_call(
        functools.partial(kernel, sizes, names),
        out_shape=(
            jax.ShapeDtypeStruct((LEVELS, WLAT, WLON, C), BF16),
            jax.ShapeDtypeStruct((r2, C), F32),
            jax.ShapeDtypeStruct((32, 2 * LANES), F32),
        ),
        in_specs=[anywhere] * 8,
        out_specs=(vmem, vmem, vmem),
        scratch_shapes=[
            pltpu.VMEM((4, LEVELS, 3, WLON, C), BF16),
            pltpu.VMEM((4, LEVELS, 3, WLON, C), BF16),
            pltpu.VMEM((C, 3 * C), BF16),
            pltpu.VMEM((C, C), BF16),
            pltpu.VMEM((1, C), F32),
            pltpu.VMEM((HEADS, RELPOS), F32),
            pltpu.VMEM(spread.shape, BF16),
            pltpu.VMEM(shares.shape, BF16),
            pltpu.VMEM((PAIRS, LANES), F32),
            pltpu.VMEM((PAIRS, LANES), F32),
            pltpu.VMEM((ROWS, LANES), F32),
            pltpu.VMEM((WIN, C), F32),
            pltpu.VMEM((WIN, C), F32),
            pltpu.VMEM((ROWS, LANES), F32),
            pltpu.VMEM((n, STACK, LANES), BF16),
            pltpu.VMEM((n, LANES, LANES), BF16),
            pltpu.VMEM((n, LANES, LANES), BF16),
            pltpu.VMEM((WIN, C), F32),
            pltpu.VMEM((ROWS, LANES), F32),
            pltpu.VMEM((WIN, 3 * C), F32),
            pltpu.VMEM((WIN, C), BF16),
            pltpu.VMEM((WIN, C), BF16),
            pltpu.VMEM((LEVELS, WLAT, WLON, C), BF16),
            pltpu.VMEM((3, LEVELS, 3, WLON, C), BF16),
            pltpu.VMEM((na, r1, C), BF16),
            pltpu.VMEM((na, r1, C), BF16),
            pltpu.VMEM((no, r2, C), BF16),
            pltpu.VMEM((no, r2, C), BF16),
            pltpu.VMEM((8, 32, 2 * LANES), BF16),
            pltpu.VMEM((no, 32, 2 * LANES), BF16),
            dma((8,)), dma((3,)), dma((3,)), dma((3,)), dma((3,)), dma(()), dma(()), dma((3,)), dma((3,)),
            dma((na,)), dma((na,)), dma((no,)), dma((no,)), dma((8,)), dma((no,)),
        ],
        compiler_params=pltpu.CompilerParams(collective_id=0, has_side_effects=True, vmem_limit_bytes=40 * 2**20),
    )(*args, spread, shares)


def per_device(sizes, names, block_inputs, cotangent, input_projection, output_projection, norm_gain, earth_bias):
    ns, na, no = sizes
    input_grad, sums, bias_sums = call_kernel(
        sizes, names, (block_inputs, cotangent, input_projection, output_projection, norm_gain, earth_bias)
    )
    lat, lon = lax.axis_index(names[1]), lax.axis_index(names[2])
    e2, x2 = 3 * C // (na * no), C // (na * no)
    entry = sums[:e2].T
    exits = sums[e2:e2 + x2].T
    gain = lax.dynamic_slice(sums[e2 + x2], ((lat * no + lon) * x2,), (x2,))
    half = WLAT * SPAN // 2
    upper, lower = bias_sums[:HEADS, :2 * half], bias_sums[16:16 + HEADS, :2 * half]
    even = jnp.concatenate([upper, lower[:, :half]], axis=1)
    odd = jnp.concatenate([upper[:, half:], lower], axis=1)
    bias = jnp.where(lon % 2 == 0, even, odd)
    return (input_grad[None], entry[None], exits[None], gain[None], bias[None, None, None])


def solution(mesh):
    names = ("section", "lat", "lon")
    sizes = tuple(mesh.shape[name] for name in names)
    in_specs = (
        P("section", None, "lat", "lon", None),
        P(None, "lat", "lon", None),
        P("section", None, None),
        P("section", None, None),
        P("section", None),
        P("section", None, "lat", None, None),
    )
    out_specs = (
        P("section", None, "lat", "lon", None),
        P("section", None, ("lat", "lon")),
        P("section", None, ("lat", "lon")),
        P("section", ("lat", "lon")),
        P("section", None, "lat", None, "lon"),
    )
    return jax.shard_map(
        functools.partial(per_device, sizes, names), mesh=mesh, in_specs=in_specs, out_specs=out_specs, check_vma=False
    )
```

```python
import functools

import jax
import jax.numpy as jnp
import numpy as np
from jax import lax
from jax.experimental import pallas as pl
from jax.experimental.pallas import tpu as pltpu
from jax.sharding import PartitionSpec as P

MESH = pl.DeviceIdType.MESH
F32 = jnp.float32
BF16 = jnp.bfloat16

C = 384
HEADS = 12
HEAD_DIM = 32
WLAT = 6
WLON = 12
LEVELS = 2
TOK = WLAT * WLON
WIN = LEVELS * TOK
SPAN = 2 * WLON - 1
RELPOS = 3312
LANES = 128
GROUPS = C // LANES
PER_GROUP = LANES // HEAD_DIM
STACK = PER_GROUP * TOK
ROWS = LEVELS * HEADS * TOK
PAIRS = LEVELS * HEADS * WLAT
EPS = 1e-05
SCALE = HEAD_DIM ** -0.5
OFF = -1e30
BIAS_ROWS = (0, 1, 3, 4)


def round_up(n, m):
    return (n + m - 1) // m * m


def spread_table():
    out = np.zeros((2 * LANES, WLON, LANES), np.float32)
    for lq in range(WLON):
        for ak in range(WLAT):
            for lk in range(WLON):
                out[ak * SPAN + lq - lk + WLON - 1, lq, ak * WLON + lk] = 1.0
    return out.reshape(2 * LANES, WLON * LANES)


def share_table(entry, exits, gains, parts, rows):
    out = np.zeros((parts, rows, entry + exits + gains), np.float32)
    e, x = entry // parts, exits // parts
    for j in range(parts):
        for r in range(e):
            out[j, r, j * e + r] = 1.0
        for r in range(x):
            out[j, e + r, entry + j * x + r] = 1.0
        out[j, e + x, entry + exits] = 1.0
    return out.reshape(parts * rows, -1)


def dot(a, b):
    return jnp.dot(a, b, preferred_element_type=F32)


def dot_t(a, b):
    return lax.dot_general(a, b, (((1,), (1,)), ((), ())), preferred_element_type=F32)


def t_dot(a, b):
    return lax.dot_general(a, b, (((0,), (0,)), ((), ())), preferred_element_type=F32)


def kernel(
    sizes, names,
    x_hbm, ct_hbm, wi_hbm, wo_hbm, gain_hbm, tab_hbm, s_hbm, p2_hbm,
    ig_out, sums_out, gain_out, bias_out,
    xin, cin, wi_v, wo_v, gain_v, tab_v, s_v, p2_v, t0, t1, bias, wide, xs, gs, att, att_t, qm, kp, vp, mixes, mix, ds, pg,
    hg, gsend, grecv, rb, sb1a, sb1b, rb1a, rb1b, sb2a, sb2b, rb2a, rb2b, bsb, brb,
    load_sem, xsend_sem, xrecv_sem, csend_sem, crecv_sem, gsend_sem, grecv_sem, bksend_sem, bkrecv_sem,
    s1send, s1recv, s2send, s2recv, bsend_sem, brecv_sem,
):
    ns, na, no = sizes
    nx = na // 2
    sec, lat, lon = (lax.axis_index(name) for name in names)
    n_sec, n_lat, n_lon = names
    lat_x, lat_y = lat // 2, lax.rem(lat, 2)

    def at_lat(k):
        return lax.rem(lat + k + na, na)

    def at_lon(k):
        return lax.rem(lon + k + no, no)

    def across(step):
        return lax.rem(lat_x + step[0], nx) * 2 + lax.rem(lat_y + step[1], 2)

    first, last = sec == 0, sec == ns - 1
    steps = [(dx, dy) for dx in range(nx) for dy in range(2) if dx or dy]
    steps.sort(key=lambda step: -(2 * min(step[0], nx - step[0]) + step[1]))
    turns = sorted(range(1, no), key=lambda k: -min(k, no - k))

    barrier = pltpu.get_barrier_semaphore()
    greeted = [{n_lon: at_lon(k)} for k in turns] + [{n_lat: across(step)} for step in steps]
    greeted += [{n_lat: at_lat(k), n_lon: at_lon(k)} for k in (-1, 1)]
    for device in greeted:
        pl.semaphore_signal(barrier, inc=1, device_id=device, device_id_type=MESH)

    @pl.when(jnp.logical_not(first))
    def _():
        pl.semaphore_signal(barrier, inc=1, device_id={n_sec: sec - 1}, device_id_type=MESH)

    @pl.when(jnp.logical_not(last))
    def _():
        pl.semaphore_signal(barrier, inc=1, device_id={n_sec: sec + 1}, device_id_type=MESH)

    halves = (pl.ds(3, 3), pl.ds(0, 3)), (pl.ds(6, 6), pl.ds(0, 6))
    quarters = ((0, 0), (0, 1), (1, 0), (1, 1))

    def quarter(ref, i):
        return ref.at[halves[0][quarters[i][0]], halves[1][quarters[i][1]]]

    loads = [
        (tab_hbm, tab_v), (s_hbm, s_v), (quarter(x_hbm, 0), xin.at[0]), (gain_hbm, gain_v),
        (wi_hbm.at[0], wi_v), (wo_hbm.at[0], wo_v), (p2_hbm, p2_v), (quarter(ct_hbm, 0), cin.at[0]),
    ]
    loads = [pltpu.make_async_copy(src, dst, load_sem.at[i]) for i, (src, dst) in enumerate(loads)]
    for copy in loads:
        copy.start()

    loads[0].wait()
    width = WLAT * SPAN
    for z in range(LEVELS):
        for a in range(WLAT):
            start = (z * 3 * WLAT + a) * width
            rows = pl.ds(z * HEADS * WLAT + a, HEADS, stride=WLAT)
            t0[rows, :] = tab_v[:, 0, start:start + LANES]
            rest = tab_v[:, 0, start + LANES:start + width]
            t1[rows, :] = jnp.concatenate([rest, jnp.zeros((HEADS, 2 * LANES - width), F32)], axis=1)
    table = jnp.concatenate([t0[...], t1[...]], axis=1)
    table_high = table.astype(BF16)
    table_low = (table - table_high.astype(F32)).astype(BF16)
    query_row = lax.rem(lax.broadcasted_iota(jnp.int32, (PAIRS, LANES), 0), WLAT)
    key = lax.broadcasted_iota(jnp.int32, (PAIRS, LANES), 1)
    apart = jnp.logical_and((query_row < 3) != (key < TOK // 2), lat == na - 1)
    closed = jnp.where(jnp.logical_or(apart, key >= TOK), OFF, 0.0)
    closed = jnp.concatenate([closed, closed], axis=1)
    loads[1].wait()
    for i in range(WLON // 2):
        spread = s_v[:, 2 * i * LANES:(2 * i + 2) * LANES]
        part = dot(table_high, spread) + dot(table_low, spread) + closed
        bias[pl.ds(2 * i, PAIRS, stride=WLON), :] = part[:, :LANES]
        bias[pl.ds(2 * i + 1, PAIRS, stride=WLON), :] = part[:, LANES:]

    pl.semaphore_wait(barrier, len(greeted) + jnp.minimum(sec, 1) + jnp.minimum(ns - 1 - sec, 1))

    def towards(i, sign):
        a, l = quarters[i]
        return ({n_lat: at_lat(sign)} if a else {}) | ({n_lon: at_lon(sign)} if l else {})

    def roll_copies(src, buffers, send, recv):
        return [
            pltpu.make_async_remote_copy(
                src_ref=quarter(src, i), dst_ref=buffers.at[i], send_sem=send.at[i], recv_sem=recv.at[i],
                device_id=towards(i, -1), device_id_type=MESH,
            )
            for i in (3, 2, 1)
        ]

    x_copies = roll_copies(x_hbm, xin, xsend_sem, xrecv_sem)
    for copy in x_copies:
        copy.start()
    c_copies = roll_copies(ct_hbm, cin, csend_sem, crecv_sem)

    @pl.when(last)
    def _():
        for copy in c_copies:
            copy.start()

    def assemble(buffers, out):
        for i, (a, l) in enumerate(quarters):
            for r in range(3):
                row = ((3 * a + r) * WLON + 6 * l) * LEVELS
                for b in range(GROUPS):
                    part = buffers[i, r, :, :, b * LANES:(b + 1) * LANES].astype(F32)
                    wide[b, row:row + 6 * LEVELS, :] = part.reshape(6 * LEVELS, LANES)
        for z in range(LEVELS):
            for b in range(GROUPS):
                rows = pl.ds(1 - z, TOK, stride=LEVELS)
                out[z * TOK:(z + 1) * TOK, b * LANES:(b + 1) * LANES] = wide[b, rows, :]

    loads[2].wait()
    for copy in x_copies:
        copy.wait_recv()
    assemble(xin, xs)
    x = xs[...]
    centered = x - jnp.mean(x, axis=-1, keepdims=True)
    inverse = lax.rsqrt(jnp.mean(centered * centered, axis=-1, keepdims=True) + EPS)
    normed = centered * inverse
    loads[3].wait()
    gain = gain_v[...]
    hidden = (normed * gain).astype(BF16)
    loads[4].wait()
    projected = dot(hidden, wi_v[...]).astype(BF16).astype(F32)

    head_of_lane = lax.broadcasted_iota(jnp.int32, (TOK, LANES), 1) // HEAD_DIM

    def stack_heads(part):
        return jnp.concatenate([jnp.where(head_of_lane == h, part, 0.0) for h in range(PER_GROUP)], axis=0)

    def unstack_heads(stacked):
        total = jnp.where(head_of_lane == 0, stacked[0:TOK], 0.0)
        for h in range(1, PER_GROUP):
            total = jnp.where(head_of_lane == h, stacked[h * TOK:(h + 1) * TOK], total)
        return total

    def pad_keys(part):
        return jnp.concatenate([part, jnp.zeros((LANES - TOK, LANES), F32)], axis=0).astype(BF16)

    def place(z, g):
        i = z * GROUPS + g
        return i, slice(z * TOK, (z + 1) * TOK), slice(g * LANES, (g + 1) * LANES), slice(i * STACK, (i + 1) * STACK)

    places = [(z, g) for z in range(LEVELS) for g in range(GROUPS)]
    for z, g in places:
        i, tokens, lanes, stacked_rows = place(z, g)
        queries = stack_heads(projected[tokens, g * LANES:(g + 1) * LANES]).astype(BF16)
        keys = pad_keys(projected[tokens, C + g * LANES:C + (g + 1) * LANES])
        values = pad_keys(projected[tokens, 2 * C + g * LANES:2 * C + (g + 1) * LANES])
        qm[i] = queries
        kp[i] = keys
        vp[i] = values
        raised = jnp.exp(dot_t(queries, keys) * SCALE + bias[stacked_rows, :])
        attention = raised / jnp.sum(raised, axis=-1, keepdims=True)
        att[stacked_rows, :] = attention
        att_t[i] = attention.T.astype(BF16)
        mixed = dot(attention.astype(BF16), values)
        mixes[stacked_rows, :] = mixed
        mix[tokens, lanes] = unstack_heads(mixed)

    loads[7].wait()

    @pl.when(last)
    def _():
        for copy in c_copies:
            copy.wait_recv()
        assemble(cin, gs)

    loads[5].wait()

    downs = [
        pltpu.make_async_remote_copy(
            src_ref=gsend.at[z], dst_ref=grecv.at[z], send_sem=gsend_sem.at[z], recv_sem=grecv_sem.at[z],
            device_id={n_sec: jnp.maximum(sec - 1, 0)}, device_id_type=MESH,
        )
        for z in range(LEVELS)
    ]
    for z in range(LEVELS):
        tokens = slice(z * TOK, (z + 1) * TOK)

        @pl.when(jnp.logical_not(last))
        def _(z=z, tokens=tokens):
            downs[z].wait_recv()
            gs[tokens, :] = grecv[z].astype(F32)[:TOK]

        grad = gs[tokens, :]
        mixed_grad = dot_t(grad.astype(BF16), wo_v[...]).astype(BF16).astype(F32)
        for g in range(GROUPS):
            i, _, lanes, stacked_rows = place(z, g)
            outer = stack_heads(mixed_grad[:, lanes])
            along = jnp.sum(outer * mixes[stacked_rows, :], axis=-1, keepdims=True)
            outer = outer.astype(BF16)
            score = att[stacked_rows, :] * (dot_t(outer, vp[i]) - along)
            ds[stacked_rows, :] = score
            score_low = score.astype(BF16)
            pg[tokens, g * LANES:(g + 1) * LANES] = unstack_heads(dot(score_low, kp[i])) * SCALE
            pg[tokens, C + g * LANES:C + (g + 1) * LANES] = t_dot(score_low, qm[i])[:TOK] * SCALE
            pg[tokens, 2 * C + g * LANES:2 * C + (g + 1) * LANES] = dot(att_t[i], outer)[:TOK]
        hidden_grad = dot_t(pg[tokens, :].astype(BF16), wi_v[...]).astype(BF16).astype(F32)
        hg[tokens, :] = hidden_grad
        normed_grad = hidden_grad * gain
        mine = normed[tokens]
        along = jnp.mean(normed_grad * mine, axis=-1, keepdims=True)
        inner = normed_grad - jnp.mean(normed_grad, axis=-1, keepdims=True) - mine * along
        input_grad = grad + inverse[tokens] * inner
        gsend[z] = jnp.concatenate([input_grad, jnp.zeros((8, C), F32)], axis=0).astype(BF16)

        @pl.when(jnp.logical_not(first))
        def _(z=z):
            downs[z].start()

        for b in range(GROUPS):
            wide[b, pl.ds(1 - z, TOK, stride=LEVELS), :] = input_grad[:, b * LANES:(b + 1) * LANES]

    for i, (a, l) in enumerate(quarters):
        for r in range(3):
            row = ((3 * a + r) * WLON + 6 * l) * LEVELS
            for b in range(GROUPS):
                part = wide[b, row:row + 6 * LEVELS, :].reshape(6, LEVELS, LANES)
                rb[i, r, :, :, b * LANES:(b + 1) * LANES] = part.astype(BF16)
    home = pltpu.make_async_copy(rb.at[0], quarter(ig_out, 0), load_sem.at[8])
    home.start()
    back_copies = [
        pltpu.make_async_remote_copy(
            src_ref=rb.at[i], dst_ref=quarter(ig_out, i), send_sem=bksend_sem.at[i], recv_sem=bkrecv_sem.at[i],
            device_id=towards(i, 1), device_id_type=MESH,
        )
        for i in (3, 2, 1)
    ]
    for copy in back_copies:
        copy.start()

    e1, x1 = 3 * C // na, C // na
    pieces = ((0, 2 * LANES, sb1a, rb1a, sb2a, rb2a), (2 * LANES, LANES, sb1b, rb1b, sb2b, rb2b))
    projected_grad = pg[...].astype(BF16)
    grad_low = gs[...].astype(BF16)
    mixed = mix[...].astype(BF16)
    gain_grad = jnp.sum(hg[...] * normed, axis=0, keepdims=True)
    gain_rows = jnp.concatenate([gain_grad, jnp.zeros((15, C), F32)], axis=0).astype(BF16)
    first_copies = []
    for p, (at, lanes, sb1, rb1, _, _) in enumerate(pieces):
        entry = t_dot(projected_grad, hidden[:, at:at + lanes]).astype(BF16)
        exits = t_dot(grad_low, mixed[:, at:at + lanes]).astype(BF16)
        for i in range(na):
            sb1[i, 0:e1] = entry[i * e1:(i + 1) * e1]
            sb1[i, e1:e1 + x1] = exits[i * x1:(i + 1) * x1]
            sb1[i, e1 + x1:e1 + x1 + 16] = gain_rows[:, at:at + lanes]
        first_copies.append([
            pltpu.make_async_remote_copy(
                src_ref=sb1.at[across(step)], dst_ref=rb1.at[2 * step[0] + step[1]],
                send_sem=s1send.at[p, 2 * step[0] + step[1]], recv_sem=s1recv.at[p, 2 * step[0] + step[1]],
                device_id={n_lat: across(step)}, device_id_type=MESH,
            )
            for step in steps
        ])
        for copy in first_copies[p]:
            copy.start()

    folded = jnp.zeros((PAIRS, 2 * LANES), F32)
    for lq in range(WLON):
        part = ds[pl.ds(lq, PAIRS, stride=WLON), :].astype(BF16)
        folded += dot_t(part, s_v[:, lq * LANES:(lq + 1) * LANES])
    t0[...] = folded[:, :LANES]
    t1[...] = folded[:, LANES:]
    quiet = jnp.zeros((16 - HEADS, 2 * LANES), F32)
    for u in range(8):
        parts = []
        for a in (BIAS_ROWS[u % 4], BIAS_ROWS[u % 4] + 1):
            rows = pl.ds(u // 4 * HEADS * WLAT + a, HEADS, stride=WLAT)
            parts += [jnp.concatenate([t0[rows, :], t1[rows, :]], axis=1), quiet]
        bsb[u] = jnp.concatenate(parts, axis=0).astype(BF16)
    if no == 16:
        def bias_copy(u, k):
            target = u if u < 4 else u + 8
            return target, pltpu.make_async_remote_copy(
                src_ref=bsb.at[u], dst_ref=brb.at[k], send_sem=bsend_sem.at[u], recv_sem=brecv_sem.at[k],
                device_id={n_lon: jnp.int32(target)}, device_id_type=MESH,
            )

        for u in range(8):
            target, copy = bias_copy(u, lon)

            @pl.when(lon != target)
            def _(copy=copy):
                copy.start()

    loads[6].wait()
    second_copies = []
    for p, (at, lanes, sb1, rb1, sb2, rb2) in enumerate(pieces):
        for copy in first_copies[p]:
            copy.wait_recv()
        total = sb1[lat].astype(F32)
        for k in range(1, na):
            total += rb1[k].astype(F32)
        sb2[...] = dot(p2_v[...], total.astype(BF16)).astype(BF16).reshape(sb2.shape)
        second_copies.append([
            pltpu.make_async_remote_copy(
                src_ref=sb2.at[at_lon(k)], dst_ref=rb2.at[k], send_sem=s2send.at[p, k], recv_sem=s2recv.at[p, k],
                device_id={n_lon: at_lon(k)}, device_id_type=MESH,
            )
            for k in turns
        ])
        for copy in second_copies[p]:
            copy.start()

    if no == 16:
        keeps = jnp.logical_or(lon < 4, lon >= 12)
        bias_out[...] = jnp.zeros_like(bias_out)

        @pl.when(keeps)
        def _():
            for s in range(no):
                @pl.when(lon != s)
                def _():
                    bias_copy(0, s)[1].wait_recv()
            brb[lon] = bsb[jnp.where(lon < 4, lon, lon - 8)]
            total = brb[0].astype(F32)
            for s in range(1, no):
                total += brb[s].astype(F32)
            upper, lower = total[:HEADS, :width], total[16:16 + HEADS, :width]
            even = jnp.concatenate([upper, lower[:, :width // 2]], axis=1)
            odd = jnp.concatenate([upper[:, width // 2:], lower], axis=1)
            bias_out[...] = jnp.where(lax.rem(lon, 2) == 0, even, odd)

        for u in range(8):
            target, copy = bias_copy(u, lon)

            @pl.when(lon != target)
            def _(copy=copy):
                copy.wait_send()
    else:
        bias_out[...] = jnp.zeros_like(bias_out)

    e2, x2 = e1 // no, x1 // no
    gains = []
    for p, (at, lanes, _, _, sb2, rb2) in enumerate(pieces):
        for copy in second_copies[p]:
            copy.wait_recv()
        total = sb2[lon].astype(F32)
        for k in range(1, no):
            total += rb2[k].astype(F32)
        sums_out[:, at:at + lanes] = total
        gains.append(total[e2 + x2:e2 + x2 + 1])

    gain_row = jnp.broadcast_to(jnp.concatenate(gains, axis=1), (8, C))
    gain_out[...] = pltpu.roll(gain_row, lax.rem(C - (lat * no + lon) * x2, C), 1)

    home.wait()
    for copy in back_copies:
        copy.wait_recv()
    for copy in x_copies + back_copies + sum(first_copies, []) + sum(second_copies, []):
        copy.wait_send()

    @pl.when(last)
    def _():
        for copy in c_copies:
            copy.wait_send()

    @pl.when(jnp.logical_not(first))
    def _():
        for copy in downs:
            copy.wait_send()


def call_kernel(sizes, names, args):
    ns, na, no = sizes
    e1, x1 = 3 * C // na, C // na
    r1 = e1 + x1 + 16
    e2, x2 = e1 // no, x1 // no
    r2 = round_up(e2 + x2 + 1, 16)
    spread = jnp.asarray(spread_table(), BF16)
    shares = jnp.asarray(share_table(e1, x1, 16, no, r2), BF16)
    hbm = pl.BlockSpec(memory_space=pltpu.HBM)
    vmem = pl.BlockSpec(memory_space=pltpu.VMEM)
    dma = pltpu.SemaphoreType.DMA
    n = LEVELS * GROUPS
    tile = (WLAT, WLON, LEVELS, C)
    parts = (4, WLAT // 2, WLON // 2, LEVELS, C)
    return pl.pallas_call(
        functools.partial(kernel, sizes, names),
        out_shape=(
            jax.ShapeDtypeStruct(tile, BF16),
            jax.ShapeDtypeStruct((r2, C), F32),
            jax.ShapeDtypeStruct((8, C), F32),
            jax.ShapeDtypeStruct((HEADS, RELPOS // 16), F32),
        ),
        in_specs=[hbm] * 8,
        out_specs=(hbm, vmem, vmem, vmem),
        scratch_shapes=[
            pltpu.VMEM(parts, BF16),
            pltpu.VMEM(parts, BF16),
            pltpu.VMEM((C, 3 * C), BF16),
            pltpu.VMEM((C, C), BF16),
            pltpu.VMEM((1, C), F32),
            pltpu.VMEM((HEADS, 1, RELPOS), F32),
            pltpu.VMEM(spread.shape, BF16),
            pltpu.VMEM(shares.shape, BF16),
            pltpu.VMEM((PAIRS, LANES), F32),
            pltpu.VMEM((PAIRS, LANES), F32),
            pltpu.VMEM((ROWS, LANES), F32),
            pltpu.VMEM((GROUPS, WIN, LANES), F32),
            pltpu.VMEM((WIN, C), F32),
            pltpu.VMEM((WIN, C), F32),
            pltpu.VMEM((ROWS, LANES), F32),
            pltpu.VMEM((n, LANES, STACK), BF16),
            pltpu.VMEM((n, STACK, LANES), BF16),
            pltpu.VMEM((n, LANES, LANES), BF16),
            pltpu.VMEM((n, LANES, LANES), BF16),
            pltpu.VMEM((ROWS, LANES), F32),
            pltpu.VMEM((WIN, C), F32),
            pltpu.VMEM((ROWS, LANES), F32),
            pltpu.VMEM((WIN, 3 * C), F32),
            pltpu.VMEM((WIN, C), F32),
            pltpu.VMEM((LEVELS, TOK + 8, C), BF16),
            pltpu.VMEM((LEVELS, TOK + 8, C), BF16),
            pltpu.VMEM(parts, BF16),
            pltpu.VMEM((na, r1, 2 * LANES), BF16),
            pltpu.VMEM((na, r1, LANES), BF16),
            pltpu.VMEM((na, r1, 2 * LANES), BF16),
            pltpu.VMEM((na, r1, LANES), BF16),
            pltpu.VMEM((no, r2, 2 * LANES), BF16),
            pltpu.VMEM((no, r2, LANES), BF16),
            pltpu.VMEM((no, r2, 2 * LANES), BF16),
            pltpu.VMEM((no, r2, LANES), BF16),
            pltpu.VMEM((8, 32, 2 * LANES), BF16),
            pltpu.VMEM((16, 32, 2 * LANES), BF16),
            dma((9,)), dma((4,)), dma((4,)), dma((4,)), dma((4,)), dma((2,)), dma((2,)), dma((4,)), dma((4,)),
            dma((2, na)), dma((2, na)), dma((2, no)), dma((2, no)), dma((8,)), dma((16,)),
        ],
        compiler_params=pltpu.CompilerParams(collective_id=0, has_side_effects=True, vmem_limit_bytes=56 * 2**20),
    )(*args, spread, shares)


def finish(share, ig_in, sums_in, gain_in, bias_in, ig_out, entry_out, exit_out, gain_out, bias_out):
    ig_out[...] = ig_in[...]
    entry_out[:, 0, :] = sums_in[0:3 * share]
    exit_out[:, 0, :] = sums_in[3 * share:4 * share]
    gain_out[...] = gain_in[0:1, 0:share]
    bias_out[:, 0, :] = bias_in[...]


def call_finish(share, *results):
    vmem = pl.BlockSpec(memory_space=pltpu.VMEM)
    return pl.pallas_call(
        functools.partial(finish, share),
        out_shape=(
            jax.ShapeDtypeStruct(results[0].shape, BF16),
            jax.ShapeDtypeStruct((3 * share, 1, C), F32),
            jax.ShapeDtypeStruct((share, 1, C), F32),
            jax.ShapeDtypeStruct((1, share), F32),
            jax.ShapeDtypeStruct((HEADS, 1, RELPOS // 16), F32),
        ),
        in_specs=[vmem] * 4,
        out_specs=(vmem,) * 5,
    )(*results)


def per_device(sizes, names, block_inputs, cotangent, input_projection, output_projection, norm_gain, earth_bias):
    ns, na, no = sizes
    args = (
        block_inputs[0].transpose(1, 2, 0, 3), cotangent.transpose(1, 2, 0, 3), input_projection, output_projection,
        norm_gain, earth_bias[0, 0, 0][:, None],
    )
    input_grad, sums, gain, bias = call_kernel(sizes, names, args)
    input_grad, entry, exits, gain, bias = call_finish(C // (na * no), input_grad, sums, gain, bias)
    return (
        input_grad.transpose(2, 0, 1, 3)[None], entry.transpose(1, 2, 0), exits.transpose(1, 2, 0), gain,
        bias[None, None].transpose(0, 1, 3, 2, 4),
    )


def solution(mesh):
    names = ("section", "lat", "lon")
    sizes = tuple(mesh.shape[name] for name in names)
    in_specs = (
        P("section", None, "lat", "lon", None),
        P(None, "lat", "lon", None),
        P("section", None, None),
        P("section", None, None),
        P("section", None),
        P("section", None, "lat", None, None),
    )
    out_specs = (
        P("section", None, "lat", "lon", None),
        P("section", None, ("lat", "lon")),
        P("section", None, ("lat", "lon")),
        P("section", ("lat", "lon")),
        P("section", None, "lat", None, "lon"),
    )
    return jax.shard_map(
        functools.partial(per_device, sizes, names), mesh=mesh, in_specs=in_specs, out_specs=out_specs, check_vma=False
    )
```

```python
import functools

import jax
import jax.numpy as jnp
import numpy as np
from jax import lax
from jax.experimental import pallas as pl
from jax.experimental.pallas import tpu as pltpu
from jax.sharding import PartitionSpec as P

MESH = pl.DeviceIdType.MESH
F32 = jnp.float32
BF16 = jnp.bfloat16

C = 384
HEADS = 12
HEAD_DIM = 32
WLAT = 6
WLON = 12
LEVELS = 2
TOK = WLAT * WLON
WIN = LEVELS * TOK
SPAN = 2 * WLON - 1
RELPOS = 3312
LANES = 128
GROUPS = C // LANES
PER_GROUP = LANES // HEAD_DIM
STACK = PER_GROUP * TOK
ROWS = LEVELS * HEADS * TOK
PAIRS = LEVELS * HEADS * WLAT
EPS = 1e-05
SCALE = HEAD_DIM ** -0.5
OFF = -1e30
BIAS_ROWS = (0, 1, 3, 4)


def round_up(n, m):
    return (n + m - 1) // m * m


def spread_table():
    out = np.zeros((2 * LANES, WLON, LANES), np.float32)
    for lq in range(WLON):
        for ak in range(WLAT):
            for lk in range(WLON):
                out[ak * SPAN + lq - lk + WLON - 1, lq, ak * WLON + lk] = 1.0
    return out.reshape(2 * LANES, WLON * LANES)


def share_table(entry, exits, gains, parts, rows):
    out = np.zeros((parts, rows, entry + exits + gains), np.float32)
    e, x = entry // parts, exits // parts
    for j in range(parts):
        for r in range(e):
            out[j, r, j * e + r] = 1.0
        for r in range(x):
            out[j, e + r, entry + j * x + r] = 1.0
        out[j, e + x, entry + exits] = 1.0
    return out.reshape(parts * rows, -1)


def dot(a, b):
    return jnp.dot(a, b, preferred_element_type=F32)


def dot_t(a, b):
    return lax.dot_general(a, b, (((1,), (1,)), ((), ())), preferred_element_type=F32)


def t_dot(a, b):
    return lax.dot_general(a, b, (((0,), (0,)), ((), ())), preferred_element_type=F32)


def kernel(
    sizes, names,
    x_hbm, ct_hbm, wi_hbm, wo_hbm, gain_hbm, tab_hbm, s_hbm, p2_hbm,
    ig_out, sums_out, gain_out, bias_out,
    xin, cin, wi_v, wo_v, gain_v, tab_v, s_v, p2_v, t0, t1, bias, wide, xs, gs, att, att_t, qm, kp, vp, mixes, mix, ds, pg,
    hg, gsend, grecv, rb, hs, hr, es, er, ms, mr, ts, tr, sb2, rb2, bsb, brb,
    load_sem, xsend_sem, xrecv_sem, csend_sem, crecv_sem, gsend_sem, grecv_sem, bksend_sem, bkrecv_sem,
    hsend_sem, hrecv_sem, esend_sem, erecv_sem, msend_sem, mrecv_sem, tsend_sem, trecv_sem, s2send, s2recv, bsend_sem, brecv_sem, go_sem,
):
    ns, na, no = sizes
    nx = na // 2
    sec, lat, lon = (lax.axis_index(name) for name in names)
    n_sec, n_lat, n_lon = names
    lat_x, lat_y = lat // 2, lax.rem(lat, 2)

    def at_lat(k):
        return lax.rem(lat + k + na, na)

    def at_lon(k):
        return lax.rem(lon + k + no, no)

    def across(step):
        return lax.rem(lat_x + step[0], nx) * 2 + lax.rem(lat_y + step[1], 2)

    def slot(step):
        return 2 * step[0] + step[1]

    first, last = sec == 0, sec == ns - 1
    steps = [(dx, dy) for dx in range(nx) for dy in range(2) if dx or dy]
    steps.sort(key=lambda step: -(2 * min(step[0], nx - step[0]) + step[1]))
    turns = sorted(range(1, no), key=lambda k: -min(k, no - k))

    barrier = pltpu.get_barrier_semaphore()
    greeted = [{n_lon: at_lon(k)} for k in turns] + [{n_lat: across(step)} for step in steps]
    greeted += [{n_lat: at_lat(k), n_lon: at_lon(k)} for k in (-1, 1)]
    for device in greeted:
        pl.semaphore_signal(barrier, inc=1, device_id=device, device_id_type=MESH)

    @pl.when(jnp.logical_not(first))
    def _():
        pl.semaphore_signal(barrier, inc=1, device_id={n_sec: sec - 1}, device_id_type=MESH)

    @pl.when(jnp.logical_not(last))
    def _():
        pl.semaphore_signal(barrier, inc=1, device_id={n_sec: sec + 1}, device_id_type=MESH)

    halves = (pl.ds(3, 3), pl.ds(0, 3)), (pl.ds(6, 6), pl.ds(0, 6))
    quarters = ((0, 0), (0, 1), (1, 0), (1, 1))

    def quarter(ref, i):
        return ref.at[halves[0][quarters[i][0]], halves[1][quarters[i][1]]]

    loads = [
        (tab_hbm, tab_v), (s_hbm, s_v), (quarter(x_hbm, 0), xin.at[0]), (gain_hbm, gain_v),
        (wi_hbm.at[0], wi_v), (wo_hbm.at[0], wo_v), (p2_hbm, p2_v), (quarter(ct_hbm, 0), cin.at[0]),
    ]
    loads = [pltpu.make_async_copy(src, dst, load_sem.at[i]) for i, (src, dst) in enumerate(loads)]
    for copy in loads:
        copy.start()

    loads[0].wait()
    width = WLAT * SPAN
    for z in range(LEVELS):
        for a in range(WLAT):
            start = (z * 3 * WLAT + a) * width
            rows = pl.ds(z * HEADS * WLAT + a, HEADS, stride=WLAT)
            t0[rows, :] = tab_v[:, 0, start:start + LANES]
            rest = tab_v[:, 0, start + LANES:start + width]
            t1[rows, :] = jnp.concatenate([rest, jnp.zeros((HEADS, 2 * LANES - width), F32)], axis=1)
    table = jnp.concatenate([t0[...], t1[...]], axis=1)
    table_high = table.astype(BF16)
    table_low = (table - table_high.astype(F32)).astype(BF16)
    query_row = lax.rem(lax.broadcasted_iota(jnp.int32, (PAIRS, LANES), 0), WLAT)
    key = lax.broadcasted_iota(jnp.int32, (PAIRS, LANES), 1)
    apart = jnp.logical_and((query_row < 3) != (key < TOK // 2), lat == na - 1)
    closed = jnp.where(jnp.logical_or(apart, key >= TOK), OFF, 0.0)
    closed = jnp.concatenate([closed, closed], axis=1)
    loads[1].wait()
    for i in range(WLON // 2):
        spread = s_v[:, 2 * i * LANES:(2 * i + 2) * LANES]
        part = dot(table_high, spread) + dot(table_low, spread) + closed
        bias[pl.ds(2 * i, PAIRS, stride=WLON), :] = part[:, :LANES]
        bias[pl.ds(2 * i + 1, PAIRS, stride=WLON), :] = part[:, LANES:]

    pl.semaphore_wait(barrier, len(greeted) + jnp.minimum(sec, 1) + jnp.minimum(ns - 1 - sec, 1))

    def towards(i, sign):
        a, l = quarters[i]
        return ({n_lat: at_lat(sign)} if a else {}) | ({n_lon: at_lon(sign)} if l else {})

    def roll_copies(src, buffers, send, recv):
        return [
            pltpu.make_async_remote_copy(
                src_ref=quarter(src, i), dst_ref=buffers.at[i], send_sem=send.at[i], recv_sem=recv.at[i],
                device_id=towards(i, -1), device_id_type=MESH,
            )
            for i in (3, 2, 1)
        ]

    x_copies = roll_copies(x_hbm, xin, xsend_sem, xrecv_sem)
    for copy in x_copies:
        copy.start()
    c_copies = roll_copies(ct_hbm, cin, csend_sem, crecv_sem)

    @pl.when(last)
    def _():
        for copy in c_copies:
            copy.start()

    def assemble(buffers, out):
        for i, (a, l) in enumerate(quarters):
            for r in range(3):
                row = ((3 * a + r) * WLON + 6 * l) * LEVELS
                for b in range(GROUPS):
                    part = buffers[i, r, :, :, b * LANES:(b + 1) * LANES].astype(F32)
                    wide[b, row:row + 6 * LEVELS, :] = part.reshape(6 * LEVELS, LANES)
        for z in range(LEVELS):
            for b in range(GROUPS):
                rows = pl.ds(1 - z, TOK, stride=LEVELS)
                out[z * TOK:(z + 1) * TOK, b * LANES:(b + 1) * LANES] = wide[b, rows, :]

    loads[2].wait()
    for copy in x_copies:
        copy.wait_recv()
    assemble(xin, xs)
    x = xs[...]
    centered = x - jnp.mean(x, axis=-1, keepdims=True)
    inverse = lax.rsqrt(jnp.mean(centered * centered, axis=-1, keepdims=True) + EPS)
    normed = centered * inverse
    loads[3].wait()
    gain = gain_v[...]
    hidden = (normed * gain).astype(BF16)
    hs[...] = hidden

    def share_copies(src, dst, send, recv, all_alike):
        return [
            pltpu.make_async_remote_copy(
                src_ref=src if all_alike else src.at[across(step)], dst_ref=dst.at[slot(step)],
                send_sem=send.at[slot(step)], recv_sem=recv.at[slot(step)],
                device_id={n_lat: across(step)}, device_id_type=MESH,
            )
            for step in steps
        ]

    hidden_copies = share_copies(hs, hr, hsend_sem, hrecv_sem, True)
    crossing = sec == ns // 2

    def send_hidden():
        for copy in hidden_copies:
            copy.start()

    pl.when(jnp.logical_not(crossing))(send_hidden)
    loads[4].wait()
    projected = dot(hidden, wi_v[...]).astype(BF16).astype(F32)

    head_of_lane = lax.broadcasted_iota(jnp.int32, (TOK, LANES), 1) // HEAD_DIM

    def stack_heads(part):
        return jnp.concatenate([jnp.where(head_of_lane == h, part, 0.0) for h in range(PER_GROUP)], axis=0)

    def unstack_heads(stacked):
        total = jnp.where(head_of_lane == 0, stacked[0:TOK], 0.0)
        for h in range(1, PER_GROUP):
            total = jnp.where(head_of_lane == h, stacked[h * TOK:(h + 1) * TOK], total)
        return total

    def pad_keys(part):
        return jnp.concatenate([part, jnp.zeros((LANES - TOK, LANES), F32)], axis=0).astype(BF16)

    def place(z, g):
        i = z * GROUPS + g
        return i, slice(z * TOK, (z + 1) * TOK), slice(g * LANES, (g + 1) * LANES), slice(i * STACK, (i + 1) * STACK)

    places = [(z, g) for z in range(LEVELS) for g in range(GROUPS)]
    for z, g in places:
        i, tokens, lanes, stacked_rows = place(z, g)
        queries = stack_heads(projected[tokens, g * LANES:(g + 1) * LANES]).astype(BF16)
        keys = pad_keys(projected[tokens, C + g * LANES:C + (g + 1) * LANES])
        values = pad_keys(projected[tokens, 2 * C + g * LANES:2 * C + (g + 1) * LANES])
        qm[i] = queries
        kp[i] = keys
        vp[i] = values
        raised = jnp.exp(dot_t(queries, keys) * SCALE + bias[stacked_rows, :])
        attention = raised / jnp.sum(raised, axis=-1, keepdims=True)
        att[stacked_rows, :] = attention
        att_t[i] = attention.T.astype(BF16)
        mixed = dot(attention.astype(BF16), values)
        mixes[stacked_rows, :] = mixed
        mix[tokens, lanes] = unstack_heads(mixed)

    loads[7].wait()

    @pl.when(last)
    def _():
        for copy in c_copies:
            copy.wait_recv()
        assemble(cin, gs)

    loads[5].wait()

    downs = [
        pltpu.make_async_remote_copy(
            src_ref=gsend.at[z], dst_ref=grecv.at[z], send_sem=gsend_sem.at[z], recv_sem=grecv_sem.at[z],
            device_id={n_sec: jnp.maximum(sec - 1, 0)}, device_id_type=MESH,
        )
        for z in range(LEVELS)
    ]
    e1, x1 = 3 * C // na, C // na
    rest = e1 % LANES
    exit_copies = share_copies(es, er, esend_sem, erecv_sem, False)

    def send_exits():
        exits = t_dot(gs[...].astype(BF16), mix[...].astype(BF16)).astype(BF16)
        for i in range(na):
            es[i] = exits[i * x1:(i + 1) * x1]
        for copy in exit_copies:
            copy.start()

    for z in range(LEVELS):
        tokens = slice(z * TOK, (z + 1) * TOK)

        @pl.when(jnp.logical_not(last))
        def _(z=z, tokens=tokens):
            downs[z].wait_recv()
            gs[tokens, :] = grecv[z].astype(F32)[:TOK]

        if z == LEVELS - 1:
            pl.when(first)(send_exits)
        grad = gs[tokens, :]
        mixed_grad = dot_t(grad.astype(BF16), wo_v[...]).astype(BF16).astype(F32)
        for g in range(GROUPS):
            i, _, lanes, stacked_rows = place(z, g)
            outer = stack_heads(mixed_grad[:, lanes])
            along = jnp.sum(outer * mixes[stacked_rows, :], axis=-1, keepdims=True)
            outer = outer.astype(BF16)
            score = att[stacked_rows, :] * (dot_t(outer, vp[i]) - along)
            ds[stacked_rows, :] = score
            score_low = score.astype(BF16)
            pg[tokens, g * LANES:(g + 1) * LANES] = unstack_heads(dot(score_low, kp[i])) * SCALE
            pg[tokens, C + g * LANES:C + (g + 1) * LANES] = t_dot(score_low, qm[i])[:TOK] * SCALE
            pg[tokens, 2 * C + g * LANES:2 * C + (g + 1) * LANES] = dot(att_t[i], outer)[:TOK]
        hidden_grad = dot_t(pg[tokens, :].astype(BF16), wi_v[...]).astype(BF16).astype(F32)
        hg[tokens, :] = hidden_grad
        normed_grad = hidden_grad * gain
        mine = normed[tokens]
        along = jnp.mean(normed_grad * mine, axis=-1, keepdims=True)
        inner = normed_grad - jnp.mean(normed_grad, axis=-1, keepdims=True) - mine * along
        input_grad = grad + inverse[tokens] * inner
        gsend[z] = jnp.concatenate([input_grad, jnp.zeros((8, C), F32)], axis=0).astype(BF16)

        @pl.when(jnp.logical_not(first))
        def _(z=z):
            downs[z].start()

        for b in range(GROUPS):
            wide[b, pl.ds(1 - z, TOK, stride=LEVELS), :] = input_grad[:, b * LANES:(b + 1) * LANES]

    if ns > 1:
        @pl.when(sec == ns - 2)
        def _():
            pl.semaphore_signal(go_sem, inc=1, device_id={n_sec: sec + 1}, device_id_type=MESH)

        @pl.when(last)
        def _():
            pl.semaphore_wait(go_sem, 1)

    pl.when(crossing)(send_hidden)
    pl.when(jnp.logical_not(first))(send_exits)
    wide_share = ms.shape[2]
    gain_grad = jnp.sum(hg[...] * normed, axis=0, keepdims=True)
    spare = round_up(C, wide_share) - C
    if spare:
        gain_grad = jnp.concatenate([gain_grad, jnp.zeros((1, spare), F32)], axis=1)
    gain_parts = [gain_grad[:, at:at + wide_share] for at in range(0, C, wide_share)]
    gain_rows = jnp.concatenate(gain_parts + [jnp.zeros((16 - len(gain_parts), wide_share), F32)], axis=0).astype(BF16)
    tails = [pg[:, (i + 1) * e1 - rest:(i + 1) * e1] for i in range(na)]
    tails = jnp.concatenate(tails, axis=1).T
    tails = jnp.concatenate([tails, jnp.zeros((na * rest, 2 * LANES - WIN), F32)], axis=1).astype(BF16)
    for i in range(na):
        ms[i, 0:WIN, :] = pg[:, i * e1:(i + 1) * e1 - rest].astype(BF16)
        ms[i, WIN:WIN + 16, :] = gain_rows
        ts[i] = tails[i * rest:(i + 1) * rest]
    share_of_grad = share_copies(ms, mr, msend_sem, mrecv_sem, False)
    tail_of_grad = share_copies(ts, tr, tsend_sem, trecv_sem, False)
    for copy, tail_copy in zip(share_of_grad, tail_of_grad):
        copy.start()
        tail_copy.start()

    for i, (a, l) in enumerate(quarters):
        for r in range(3):
            row = ((3 * a + r) * WLON + 6 * l) * LEVELS
            for b in range(GROUPS):
                part = wide[b, row:row + 6 * LEVELS, :].reshape(6, LEVELS, LANES)
                rb[i, r, :, :, b * LANES:(b + 1) * LANES] = part.astype(BF16)
    home = pltpu.make_async_copy(rb.at[0], quarter(ig_out, 0), load_sem.at[8])
    home.start()
    back_copies = [
        pltpu.make_async_remote_copy(
            src_ref=rb.at[i], dst_ref=quarter(ig_out, i), send_sem=bksend_sem.at[i], recv_sem=bkrecv_sem.at[i],
            device_id=towards(i, 1), device_id_type=MESH,
        )
        for i in (3, 2, 1)
    ]
    for copy in back_copies:
        copy.start()

    folded = jnp.zeros((PAIRS, 2 * LANES), F32)
    for lq in range(WLON):
        part = ds[pl.ds(lq, PAIRS, stride=WLON), :].astype(BF16)
        folded += dot_t(part, s_v[:, lq * LANES:(lq + 1) * LANES])
    t0[...] = folded[:, :LANES]
    t1[...] = folded[:, LANES:]
    for u in range(8):
        upper, lower = (
            jnp.concatenate([t0[rows, :], t1[rows, :]], axis=1)
            for rows in (pl.ds(u // 4 * HEADS * WLAT + BIAS_ROWS[u % 4] + k, HEADS, stride=WLAT) for k in range(2))
        )
        half = width // 2
        if u % 2 == 0:
            lower = lower[:, :half]
        else:
            upper, lower = upper[:, half:width], lower[:, :width]
        both = jnp.concatenate([upper[:, :width], lower, jnp.zeros((HEADS, 2 * LANES - RELPOS // 16), F32)], axis=1)
        bsb[u] = jnp.concatenate([both, jnp.zeros((16 - HEADS, 2 * LANES), F32)], axis=0).astype(BF16)
    if no == 16:
        def bias_copy(u, k):
            target = u if u < 4 else u + 8
            return target, pltpu.make_async_remote_copy(
                src_ref=bsb.at[u], dst_ref=brb.at[k], send_sem=bsend_sem.at[u], recv_sem=brecv_sem.at[k],
                device_id={n_lon: jnp.int32(target)}, device_id_type=MESH,
            )

        for u in range(8):
            target, copy = bias_copy(u, lon)

            @pl.when(lon != target)
            def _(copy=copy):
                copy.start()

    loads[6].wait()
    own = ms[lat]
    entry = t_dot(own[:WIN], hidden)
    entry_tail = dot(ts[lat][:, :WIN], hidden)
    exits = es[lat].astype(F32)
    gain_total = own[WIN:WIN + 16].astype(F32)
    for i in reversed(range(len(steps))):
        k = slot(steps[i])
        for copies in (hidden_copies, exit_copies, share_of_grad, tail_of_grad):
            copies[i].wait_recv()
        entry += t_dot(mr[k][:WIN], hr[k])
        entry_tail += dot(tr[k][:, :WIN], hr[k])
        exits += er[k].astype(F32)
        gain_total += mr[k][WIN:WIN + 16].astype(F32)
    gain_total = jnp.concatenate([gain_total[i:i + 1] for i in range(len(gain_parts))], axis=1)[:, :C]
    total = jnp.concatenate([entry, entry_tail, exits, gain_total, jnp.zeros((15, C), F32)], axis=0)
    sb2[...] = dot(p2_v[...], total.astype(BF16)).astype(BF16).reshape(sb2.shape)
    second_copies = [
        pltpu.make_async_remote_copy(
            src_ref=sb2.at[at_lon(k)], dst_ref=rb2.at[k], send_sem=s2send.at[k], recv_sem=s2recv.at[k],
            device_id={n_lon: at_lon(k)}, device_id_type=MESH,
        )
        for k in turns
    ]
    for copy in second_copies:
        copy.start()

    if no == 16:
        keeps = jnp.logical_or(lon < 4, lon >= 12)
        bias_out[...] = jnp.zeros_like(bias_out)

        @pl.when(keeps)
        def _():
            for s in range(no):
                @pl.when(lon != s)
                def _():
                    bias_copy(0, s)[1].wait_recv()
            brb[lon] = bsb[jnp.where(lon < 4, lon, lon - 8)]
            total = brb[0].astype(F32)
            for s in range(1, no):
                total += brb[s].astype(F32)
            bias_out[...] = total[:HEADS, :RELPOS // 16]

        for u in range(8):
            target, copy = bias_copy(u, lon)

            @pl.when(lon != target)
            def _(copy=copy):
                copy.wait_send()
    else:
        bias_out[...] = jnp.zeros_like(bias_out)

    e2, x2 = e1 // no, x1 // no
    for copy in second_copies:
        copy.wait_recv()
    total = sb2[lon].astype(F32)
    for k in range(1, no):
        total += rb2[k].astype(F32)
    sums_out[...] = total
    gain_row = jnp.broadcast_to(total[e2 + x2:e2 + x2 + 1], (8, C))
    gain_out[...] = pltpu.roll(gain_row, lax.rem(C - (lat * no + lon) * x2, C), 1)

    home.wait()
    for copy in back_copies:
        copy.wait_recv()
    for copy in x_copies + back_copies + hidden_copies + exit_copies + share_of_grad + tail_of_grad + second_copies:
        copy.wait_send()

    @pl.when(last)
    def _():
        for copy in c_copies:
            copy.wait_send()

    @pl.when(jnp.logical_not(first))
    def _():
        for copy in downs:
            copy.wait_send()


def call_kernel(sizes, names, args):
    ns, na, no = sizes
    e1, x1 = 3 * C // na, C // na
    e2, x2 = e1 // no, x1 // no
    r2 = round_up(e2 + x2 + 1, 16)
    spread = jnp.asarray(spread_table(), BF16)
    shares = jnp.asarray(share_table(e1, x1, 16, no, r2), BF16)
    hbm = pl.BlockSpec(memory_space=pltpu.HBM)
    vmem = pl.BlockSpec(memory_space=pltpu.VMEM)
    dma = pltpu.SemaphoreType.DMA
    n = LEVELS * GROUPS
    tile = (WLAT, WLON, LEVELS, C)
    parts = (4, WLAT // 2, WLON // 2, LEVELS, C)
    return pl.pallas_call(
        functools.partial(kernel, sizes, names),
        out_shape=(
            jax.ShapeDtypeStruct(tile, BF16),
            jax.ShapeDtypeStruct((r2, C), F32),
            jax.ShapeDtypeStruct((8, C), F32),
            jax.ShapeDtypeStruct((HEADS, RELPOS // 16), F32),
        ),
        in_specs=[hbm] * 8,
        out_specs=(hbm, vmem, vmem, vmem),
        scratch_shapes=[
            pltpu.VMEM(parts, BF16),
            pltpu.VMEM(parts, BF16),
            pltpu.VMEM((C, 3 * C), BF16),
            pltpu.VMEM((C, C), BF16),
            pltpu.VMEM((1, C), F32),
            pltpu.VMEM((HEADS, 1, RELPOS), F32),
            pltpu.VMEM(spread.shape, BF16),
            pltpu.VMEM(shares.shape, BF16),
            pltpu.VMEM((PAIRS, LANES), F32),
            pltpu.VMEM((PAIRS, LANES), F32),
            pltpu.VMEM((ROWS, LANES), F32),
            pltpu.VMEM((GROUPS, WIN, LANES), F32),
            pltpu.VMEM((WIN, C), F32),
            pltpu.VMEM((WIN, C), F32),
            pltpu.VMEM((ROWS, LANES), F32),
            pltpu.VMEM((n, LANES, STACK), BF16),
            pltpu.VMEM((n, STACK, LANES), BF16),
            pltpu.VMEM((n, LANES, LANES), BF16),
            pltpu.VMEM((n, LANES, LANES), BF16),
            pltpu.VMEM((ROWS, LANES), F32),
            pltpu.VMEM((WIN, C), F32),
            pltpu.VMEM((ROWS, LANES), F32),
            pltpu.VMEM((WIN, 3 * C), F32),
            pltpu.VMEM((WIN, C), F32),
            pltpu.VMEM((LEVELS, TOK + 8, C), BF16),
            pltpu.VMEM((LEVELS, TOK + 8, C), BF16),
            pltpu.VMEM(parts, BF16),
            pltpu.VMEM((WIN, C), BF16),
            pltpu.VMEM((na, WIN, C), BF16),
            pltpu.VMEM((na, x1, C), BF16),
            pltpu.VMEM((na, x1, C), BF16),
            pltpu.VMEM((na, WIN + 16, e1 - e1 % LANES), BF16),
            pltpu.VMEM((na, WIN + 16, e1 - e1 % LANES), BF16),
            pltpu.VMEM((na, e1 % LANES, 2 * LANES), BF16),
            pltpu.VMEM((na, e1 % LANES, 2 * LANES), BF16),
            pltpu.VMEM((no, r2, C), BF16),
            pltpu.VMEM((no, r2, C), BF16),
            pltpu.VMEM((8, 16, 2 * LANES), BF16),
            pltpu.VMEM((16, 16, 2 * LANES), BF16),
            dma((9,)), dma((4,)), dma((4,)), dma((4,)), dma((4,)), dma((2,)), dma((2,)), dma((4,)), dma((4,)),
            dma((na,)), dma((na,)), dma((na,)), dma((na,)), dma((na,)), dma((na,)), dma((na,)), dma((na,)), dma((no,)), dma((no,)), dma((8,)), dma((16,)),
            pltpu.SemaphoreType.REGULAR,
        ],
        compiler_params=pltpu.CompilerParams(collective_id=0, has_side_effects=True, vmem_limit_bytes=56 * 2**20),
    )(*args, spread, shares)


def finish(share, ig_in, sums_in, gain_in, bias_in, ig_out, entry_out, exit_out, gain_out, bias_out):
    ig_out[...] = ig_in[...]
    entry_out[:, 0, :] = sums_in[0:3 * share]
    exit_out[:, 0, :] = sums_in[3 * share:4 * share]
    gain_out[...] = gain_in[0:1, 0:share]
    bias_out[:, 0, :] = bias_in[...]


def call_finish(share, *results):
    vmem = pl.BlockSpec(memory_space=pltpu.VMEM)
    return pl.pallas_call(
        functools.partial(finish, share),
        out_shape=(
            jax.ShapeDtypeStruct(results[0].shape, BF16),
            jax.ShapeDtypeStruct((3 * share, 1, C), F32),
            jax.ShapeDtypeStruct((share, 1, C), F32),
            jax.ShapeDtypeStruct((1, share), F32),
            jax.ShapeDtypeStruct((HEADS, 1, RELPOS // 16), F32),
        ),
        in_specs=[vmem] * 4,
        out_specs=(vmem,) * 5,
    )(*results)


def per_device(sizes, names, block_inputs, cotangent, input_projection, output_projection, norm_gain, earth_bias):
    ns, na, no = sizes
    args = (
        block_inputs[0].transpose(1, 2, 0, 3), cotangent.transpose(1, 2, 0, 3), input_projection, output_projection,
        norm_gain, earth_bias[0, 0, 0][:, None],
    )
    input_grad, sums, gain, bias = call_kernel(sizes, names, args)
    input_grad, entry, exits, gain, bias = call_finish(C // (na * no), input_grad, sums, gain, bias)
    return (
        input_grad.transpose(2, 0, 1, 3)[None], entry.transpose(1, 2, 0), exits.transpose(1, 2, 0), gain,
        bias[None, None].transpose(0, 1, 3, 2, 4),
    )


def solution(mesh):
    names = ("section", "lat", "lon")
    sizes = tuple(mesh.shape[name] for name in names)
    in_specs = (
        P("section", None, "lat", "lon", None),
        P(None, "lat", "lon", None),
        P("section", None, None),
        P("section", None, None),
        P("section", None),
        P("section", None, "lat", None, None),
    )
    out_specs = (
        P("section", None, "lat", "lon", None),
        P("section", None, ("lat", "lon")),
        P("section", None, ("lat", "lon")),
        P("section", ("lat", "lon")),
        P("section", None, "lat", None, "lon"),
    )
    return jax.shard_map(
        functools.partial(per_device, sizes, names), mesh=mesh, in_specs=in_specs, out_specs=out_specs, check_vma=False
    )
```

```python
import functools

import jax
import jax.numpy as jnp
import numpy as np
from jax import lax
from jax.experimental import pallas as pl
from jax.experimental.pallas import tpu as pltpu
from jax.sharding import PartitionSpec as P

MESH = pl.DeviceIdType.MESH
F32 = jnp.float32
BF16 = jnp.bfloat16

C = 384
HEADS = 12
HEAD_DIM = 32
WLAT = 6
WLON = 12
LEVELS = 2
TOK = WLAT * WLON
WIN = LEVELS * TOK
SPAN = 2 * WLON - 1
RELPOS = 3312
LANES = 128
GROUPS = C // LANES
PER_GROUP = LANES // HEAD_DIM
STACK = PER_GROUP * TOK
ROWS = LEVELS * HEADS * TOK
PAIRS = LEVELS * HEADS * WLAT
EPS = 1e-05
SCALE = HEAD_DIM ** -0.5
OFF = -1e30
BIAS_ROWS = (0, 1, 3, 4)


def round_up(n, m):
    return (n + m - 1) // m * m


def spread_table():
    out = np.zeros((2 * LANES, WLON, LANES), np.float32)
    for lq in range(WLON):
        for ak in range(WLAT):
            for lk in range(WLON):
                out[ak * SPAN + lq - lk + WLON - 1, lq, ak * WLON + lk] = 1.0
    return out.reshape(2 * LANES, WLON * LANES)


def share_table(entry, exits, gains, parts, rows):
    out = np.zeros((parts, rows, entry + exits + gains), np.float32)
    e, x = entry // parts, exits // parts
    for j in range(parts):
        for r in range(e):
            out[j, r, j * e + r] = 1.0
        for r in range(x):
            out[j, e + r, entry + j * x + r] = 1.0
        out[j, e + x, entry + exits] = 1.0
    return out.reshape(parts * rows, -1)


def dot(a, b):
    return jnp.dot(a, b, preferred_element_type=F32)


def dot_t(a, b):
    return lax.dot_general(a, b, (((1,), (1,)), ((), ())), preferred_element_type=F32)


def t_dot(a, b):
    return lax.dot_general(a, b, (((0,), (0,)), ((), ())), preferred_element_type=F32)


def kernel(
    sizes, names,
    x_hbm, ct_hbm, wi_hbm, wo_hbm, gain_hbm, tab_hbm, s_hbm, p2_hbm,
    ig_out, sums_out, gain_out, bias_out,
    xin, cin, wi_v, wo_v, gain_v, tab_v, s_v, p2_v, t0, t1, bias, wide, xs, gs, att, att_t, qm, kp, vp, mixes, mix, ds, pg,
    hg, gsend, grecv, rb, hs, hr, es, er, ms, mr, ts, tr, sb2, rb2, bsb, brb,
    load_sem, xsend_sem, xrecv_sem, csend_sem, crecv_sem, gsend_sem, grecv_sem, bksend_sem, bkrecv_sem,
    hsend_sem, hrecv_sem, esend_sem, erecv_sem, msend_sem, mrecv_sem, tsend_sem, trecv_sem, s2send, s2recv, bsend_sem, brecv_sem,
):
    ns, na, no = sizes
    nx = na // 2
    sec, lat, lon = (lax.axis_index(name) for name in names)
    n_sec, n_lat, n_lon = names
    lat_x, lat_y = lat // 2, lax.rem(lat, 2)

    def at_lat(k):
        return lax.rem(lat + k + na, na)

    def at_lon(k):
        return lax.rem(lon + k + no, no)

    def across(step):
        return lax.rem(lat_x + step[0], nx) * 2 + lax.rem(lat_y + step[1], 2)

    def slot(step):
        return 2 * step[0] + step[1]

    first, last = sec == 0, sec == ns - 1
    steps = [(dx, dy) for dx in range(nx) for dy in range(2) if dx or dy]
    steps.sort(key=lambda step: -(2 * min(step[0], nx - step[0]) + step[1]))
    turns = sorted(range(1, no), key=lambda k: -min(k, no - k))

    barrier = pltpu.get_barrier_semaphore()
    greeted = [{n_lon: at_lon(k)} for k in turns] + [{n_lat: across(step)} for step in steps]
    greeted += [{n_lat: at_lat(k), n_lon: at_lon(k)} for k in (-1, 1)]
    for device in greeted:
        pl.semaphore_signal(barrier, inc=1, device_id=device, device_id_type=MESH)

    @pl.when(jnp.logical_not(first))
    def _():
        pl.semaphore_signal(barrier, inc=1, device_id={n_sec: sec - 1}, device_id_type=MESH)

    @pl.when(jnp.logical_not(last))
    def _():
        pl.semaphore_signal(barrier, inc=1, device_id={n_sec: sec + 1}, device_id_type=MESH)

    halves = (pl.ds(3, 3), pl.ds(0, 3)), (pl.ds(6, 6), pl.ds(0, 6))
    quarters = ((0, 0), (0, 1), (1, 0), (1, 1))

    def quarter(ref, i):
        return ref.at[halves[0][quarters[i][0]], halves[1][quarters[i][1]]]

    loads = [
        (tab_hbm, tab_v), (s_hbm, s_v), (quarter(x_hbm, 0), xin.at[0]), (gain_hbm, gain_v),
        (wi_hbm.at[0], wi_v), (wo_hbm.at[0], wo_v), (p2_hbm, p2_v), (quarter(ct_hbm, 0), cin.at[0]),
    ]
    loads = [pltpu.make_async_copy(src, dst, load_sem.at[i]) for i, (src, dst) in enumerate(loads)]
    for copy in loads:
        copy.start()

    loads[0].wait()
    width = WLAT * SPAN
    for z in range(LEVELS):
        for a in range(WLAT):
            start = (z * 3 * WLAT + a) * width
            rows = pl.ds(z * HEADS * WLAT + a, HEADS, stride=WLAT)
            t0[rows, :] = tab_v[:, 0, start:start + LANES]
            rest = tab_v[:, 0, start + LANES:start + width]
            t1[rows, :] = jnp.concatenate([rest, jnp.zeros((HEADS, 2 * LANES - width), F32)], axis=1)
    table = jnp.concatenate([t0[...], t1[...]], axis=1)
    table_high = table.astype(BF16)
    table_low = (table - table_high.astype(F32)).astype(BF16)
    query_row = lax.rem(lax.broadcasted_iota(jnp.int32, (PAIRS, LANES), 0), WLAT)
    key = lax.broadcasted_iota(jnp.int32, (PAIRS, LANES), 1)
    apart = jnp.logical_and((query_row < 3) != (key < TOK // 2), lat == na - 1)
    closed = jnp.where(jnp.logical_or(apart, key >= TOK), OFF, 0.0)
    closed = jnp.concatenate([closed, closed], axis=1)
    loads[1].wait()
    for i in range(WLON // 2):
        spread = s_v[:, 2 * i * LANES:(2 * i + 2) * LANES]
        part = dot(table_high, spread) + dot(table_low, spread) + closed
        bias[pl.ds(2 * i, PAIRS, stride=WLON), :] = part[:, :LANES]
        bias[pl.ds(2 * i + 1, PAIRS, stride=WLON), :] = part[:, LANES:]

    pl.semaphore_wait(barrier, len(greeted) + jnp.minimum(sec, 1) + jnp.minimum(ns - 1 - sec, 1))

    def towards(i, sign):
        a, l = quarters[i]
        return ({n_lat: at_lat(sign)} if a else {}) | ({n_lon: at_lon(sign)} if l else {})

    def roll_copies(src, buffers, send, recv):
        return [
            pltpu.make_async_remote_copy(
                src_ref=quarter(src, i), dst_ref=buffers.at[i], send_sem=send.at[i], recv_sem=recv.at[i],
                device_id=towards(i, -1), device_id_type=MESH,
            )
            for i in (3, 2, 1)
        ]

    x_copies = roll_copies(x_hbm, xin, xsend_sem, xrecv_sem)
    for copy in x_copies:
        copy.start()
    c_copies = roll_copies(ct_hbm, cin, csend_sem, crecv_sem)

    @pl.when(last)
    def _():
        for copy in c_copies:
            copy.start()

    def assemble(buffers, out):
        for i, (a, l) in enumerate(quarters):
            for r in range(3):
                row = ((3 * a + r) * WLON + 6 * l) * LEVELS
                for b in range(GROUPS):
                    part = buffers[i, r, :, :, b * LANES:(b + 1) * LANES].astype(F32)
                    wide[b, row:row + 6 * LEVELS, :] = part.reshape(6 * LEVELS, LANES)
        for z in range(LEVELS):
            for b in range(GROUPS):
                rows = pl.ds(1 - z, TOK, stride=LEVELS)
                out[z * TOK:(z + 1) * TOK, b * LANES:(b + 1) * LANES] = wide[b, rows, :]

    loads[2].wait()
    for copy in x_copies:
        copy.wait_recv()
    assemble(xin, xs)
    x = xs[...]
    centered = x - jnp.mean(x, axis=-1, keepdims=True)
    inverse = lax.rsqrt(jnp.mean(centered * centered, axis=-1, keepdims=True) + EPS)
    normed = centered * inverse
    loads[3].wait()
    gain = gain_v[...]
    hidden = (normed * gain).astype(BF16)
    hs[...] = hidden

    def share_copies(src, dst, send, recv):
        return [
            pltpu.make_async_remote_copy(
                src_ref=src.at[across(step)], dst_ref=dst.at[slot(step)],
                send_sem=send.at[slot(step)], recv_sem=recv.at[slot(step)],
                device_id={n_lat: across(step)}, device_id_type=MESH,
            )
            for step in steps
        ]

    hidden_copies = []
    for step in steps:
        through = step[0] and step[1]
        hidden_copies.append(pltpu.make_async_remote_copy(
            src_ref=hr.at[1] if through else hs, dst_ref=hr.at[slot(step)],
            send_sem=hsend_sem.at[slot(step)], recv_sem=hrecv_sem.at[slot(step)],
            device_id={n_lat: across((step[0], 0) if through else step)}, device_id_type=MESH,
        ))
    hidden_copies[steps.index((0, 1))].start()

    def pass_hidden():
        hidden_copies[steps.index((0, 1))].wait_recv()
        for step, copy in zip(steps, hidden_copies):
            if step[0]:
                copy.start()

    loads[4].wait()
    projected = dot(hidden, wi_v[...]).astype(BF16).astype(F32)

    head_of_lane = lax.broadcasted_iota(jnp.int32, (TOK, LANES), 1) // HEAD_DIM

    def stack_heads(part):
        return jnp.concatenate([jnp.where(head_of_lane == h, part, 0.0) for h in range(PER_GROUP)], axis=0)

    def unstack_heads(stacked):
        total = jnp.where(head_of_lane == 0, stacked[0:TOK], 0.0)
        for h in range(1, PER_GROUP):
            total = jnp.where(head_of_lane == h, stacked[h * TOK:(h + 1) * TOK], total)
        return total

    def pad_keys(part):
        return jnp.concatenate([part, jnp.zeros((LANES - TOK, LANES), F32)], axis=0).astype(BF16)

    def place(z, g):
        i = z * GROUPS + g
        return i, slice(z * TOK, (z + 1) * TOK), slice(g * LANES, (g + 1) * LANES), slice(i * STACK, (i + 1) * STACK)

    places = [(z, g) for z in range(LEVELS) for g in range(GROUPS)]
    for z, g in places:
        i, tokens, lanes, stacked_rows = place(z, g)
        queries = stack_heads(projected[tokens, g * LANES:(g + 1) * LANES]).astype(BF16)
        keys = pad_keys(projected[tokens, C + g * LANES:C + (g + 1) * LANES])
        values = pad_keys(projected[tokens, 2 * C + g * LANES:2 * C + (g + 1) * LANES])
        qm[i] = queries
        kp[i] = keys
        vp[i] = values
        raised = jnp.exp(dot_t(queries, keys) * SCALE + bias[stacked_rows, :])
        attention = raised / jnp.sum(raised, axis=-1, keepdims=True)
        att[stacked_rows, :] = attention
        att_t[i] = attention.T.astype(BF16)
        mixed = dot(attention.astype(BF16), values)
        mixes[stacked_rows, :] = mixed
        mix[tokens, lanes] = unstack_heads(mixed)
    pass_hidden()

    loads[7].wait()

    @pl.when(last)
    def _():
        for copy in c_copies:
            copy.wait_recv()
        assemble(cin, gs)

    loads[5].wait()

    downs = [
        pltpu.make_async_remote_copy(
            src_ref=gsend.at[z], dst_ref=grecv.at[z], send_sem=gsend_sem.at[z], recv_sem=grecv_sem.at[z],
            device_id={n_sec: jnp.maximum(sec - 1, 0)}, device_id_type=MESH,
        )
        for z in range(LEVELS)
    ]
    e1, x1 = 3 * C // na, C // na
    rest = e1 % LANES
    exit_copies = share_copies(es, er, esend_sem, erecv_sem)

    def send_exits():
        exits = t_dot(gs[...].astype(BF16), mix[...].astype(BF16)).astype(BF16)
        for i in range(na):
            es[i] = exits[i * x1:(i + 1) * x1]
        for copy in exit_copies:
            copy.start()

    for z in range(LEVELS):
        tokens = slice(z * TOK, (z + 1) * TOK)

        @pl.when(jnp.logical_not(last))
        def _(z=z, tokens=tokens):
            downs[z].wait_recv()
            gs[tokens, :] = grecv[z].astype(F32)[:TOK]

        if z == LEVELS - 1:
            pl.when(sec < ns // 2)(send_exits)
        grad = gs[tokens, :]
        mixed_grad = dot_t(grad.astype(BF16), wo_v[...]).astype(BF16).astype(F32)
        for g in range(GROUPS):
            i, _, lanes, stacked_rows = place(z, g)
            outer = stack_heads(mixed_grad[:, lanes])
            along = jnp.sum(outer * mixes[stacked_rows, :], axis=-1, keepdims=True)
            outer = outer.astype(BF16)
            score = att[stacked_rows, :] * (dot_t(outer, vp[i]) - along)
            ds[stacked_rows, :] = score
            score_low = score.astype(BF16)
            pg[tokens, g * LANES:(g + 1) * LANES] = unstack_heads(dot(score_low, kp[i])) * SCALE
            pg[tokens, C + g * LANES:C + (g + 1) * LANES] = t_dot(score_low, qm[i])[:TOK] * SCALE
            pg[tokens, 2 * C + g * LANES:2 * C + (g + 1) * LANES] = dot(att_t[i], outer)[:TOK]
        hidden_grad = dot_t(pg[tokens, :].astype(BF16), wi_v[...]).astype(BF16).astype(F32)
        hg[tokens, :] = hidden_grad
        normed_grad = hidden_grad * gain
        mine = normed[tokens]
        along = jnp.mean(normed_grad * mine, axis=-1, keepdims=True)
        inner = normed_grad - jnp.mean(normed_grad, axis=-1, keepdims=True) - mine * along
        input_grad = grad + inverse[tokens] * inner
        gsend[z] = jnp.concatenate([input_grad, jnp.zeros((8, C), F32)], axis=0).astype(BF16)

        @pl.when(jnp.logical_not(first))
        def _(z=z):
            downs[z].start()

        for b in range(GROUPS):
            wide[b, pl.ds(1 - z, TOK, stride=LEVELS), :] = input_grad[:, b * LANES:(b + 1) * LANES]

    wide_share = ms.shape[2]
    gain_grad = jnp.sum(hg[...] * normed, axis=0, keepdims=True)
    spare = round_up(C, wide_share) - C
    if spare:
        gain_grad = jnp.concatenate([gain_grad, jnp.zeros((1, spare), F32)], axis=1)
    gain_parts = [gain_grad[:, at:at + wide_share] for at in range(0, C, wide_share)]
    gain_rows = jnp.concatenate(gain_parts + [jnp.zeros((16 - len(gain_parts), wide_share), F32)], axis=0).astype(BF16)
    tails = [pg[:, (i + 1) * e1 - rest:(i + 1) * e1] for i in range(na)]
    tails = jnp.concatenate(tails, axis=1).T
    tails = jnp.concatenate([tails, jnp.zeros((na * rest, 2 * LANES - WIN), F32)], axis=1).astype(BF16)
    for i in range(na):
        ms[i, 0:WIN, :] = pg[:, i * e1:(i + 1) * e1 - rest].astype(BF16)
        ms[i, WIN:WIN + 16, :] = gain_rows
        ts[i] = tails[i * rest:(i + 1) * rest]
    share_of_grad = share_copies(ms, mr, msend_sem, mrecv_sem)
    tail_of_grad = share_copies(ts, tr, tsend_sem, trecv_sem)
    for copy, tail_copy in zip(share_of_grad, tail_of_grad):
        copy.start()
        tail_copy.start()
    pl.when(sec >= ns // 2)(send_exits)

    for i, (a, l) in enumerate(quarters):
        for r in range(3):
            row = ((3 * a + r) * WLON + 6 * l) * LEVELS
            for b in range(GROUPS):
                part = wide[b, row:row + 6 * LEVELS, :].reshape(6, LEVELS, LANES)
                rb[i, r, :, :, b * LANES:(b + 1) * LANES] = part.astype(BF16)
    home = pltpu.make_async_copy(rb.at[0], quarter(ig_out, 0), load_sem.at[8])
    home.start()
    back_copies = [
        pltpu.make_async_remote_copy(
            src_ref=rb.at[i], dst_ref=quarter(ig_out, i), send_sem=bksend_sem.at[i], recv_sem=bkrecv_sem.at[i],
            device_id=towards(i, 1), device_id_type=MESH,
        )
        for i in (3, 2, 1)
    ]
    for copy in back_copies:
        copy.start()

    folded = jnp.zeros((PAIRS, 2 * LANES), F32)
    for lq in range(WLON):
        part = ds[pl.ds(lq, PAIRS, stride=WLON), :].astype(BF16)
        folded += dot_t(part, s_v[:, lq * LANES:(lq + 1) * LANES])
    t0[...] = folded[:, :LANES]
    t1[...] = folded[:, LANES:]
    for u in range(8):
        upper, lower = (
            jnp.concatenate([t0[rows, :], t1[rows, :]], axis=1)
            for rows in (pl.ds(u // 4 * HEADS * WLAT + BIAS_ROWS[u % 4] + k, HEADS, stride=WLAT) for k in range(2))
        )
        half = width // 2
        if u % 2 == 0:
            lower = lower[:, :half]
        else:
            upper, lower = upper[:, half:width], lower[:, :width]
        both = jnp.concatenate([upper[:, :width], lower, jnp.zeros((HEADS, 2 * LANES - RELPOS // 16), F32)], axis=1)
        bsb[u] = jnp.concatenate([both, jnp.zeros((16 - HEADS, 2 * LANES), F32)], axis=0).astype(BF16)
    if no == 16:
        def bias_copy(u, k):
            target = u if u < 4 else u + 8
            return target, pltpu.make_async_remote_copy(
                src_ref=bsb.at[u], dst_ref=brb.at[k], send_sem=bsend_sem.at[u], recv_sem=brecv_sem.at[k],
                device_id={n_lon: jnp.int32(target)}, device_id_type=MESH,
            )

        for u in range(8):
            target, copy = bias_copy(u, lon)

            @pl.when(lon != target)
            def _(copy=copy):
                copy.start()

    loads[6].wait()
    own = ms[lat]
    entry = t_dot(own[:WIN], hidden)
    entry_tail = dot(ts[lat][:, :WIN], hidden)
    exits = es[lat].astype(F32)
    gain_total = own[WIN:WIN + 16].astype(F32)
    for i in reversed(range(len(steps))):
        k = slot(steps[i])
        if steps[i] != (0, 1):
            hidden_copies[i].wait_recv()
        for copies in (exit_copies, share_of_grad, tail_of_grad):
            copies[i].wait_recv()
        entry += t_dot(mr[k][:WIN], hr[k])
        entry_tail += dot(tr[k][:, :WIN], hr[k])
        exits += er[k].astype(F32)
        gain_total += mr[k][WIN:WIN + 16].astype(F32)
    gain_total = jnp.concatenate([gain_total[i:i + 1] for i in range(len(gain_parts))], axis=1)[:, :C]
    total = jnp.concatenate([entry, entry_tail, exits, gain_total, jnp.zeros((15, C), F32)], axis=0)
    sb2[...] = dot(p2_v[...], total.astype(BF16)).astype(BF16).reshape(sb2.shape)
    second_copies = [
        pltpu.make_async_remote_copy(
            src_ref=sb2.at[at_lon(k)], dst_ref=rb2.at[k], send_sem=s2send.at[k], recv_sem=s2recv.at[k],
            device_id={n_lon: at_lon(k)}, device_id_type=MESH,
        )
        for k in turns
    ]
    for copy in second_copies:
        copy.start()

    if no == 16:
        keeps = jnp.logical_or(lon < 4, lon >= 12)
        bias_out[...] = jnp.zeros_like(bias_out)

        @pl.when(keeps)
        def _():
            for s in range(no):
                @pl.when(lon != s)
                def _():
                    bias_copy(0, s)[1].wait_recv()
            brb[lon] = bsb[jnp.where(lon < 4, lon, lon - 8)]
            total = brb[0].astype(F32)
            for s in range(1, no):
                total += brb[s].astype(F32)
            bias_out[...] = total[:HEADS, :RELPOS // 16]

        for u in range(8):
            target, copy = bias_copy(u, lon)

            @pl.when(lon != target)
            def _(copy=copy):
                copy.wait_send()
    else:
        bias_out[...] = jnp.zeros_like(bias_out)

    e2, x2 = e1 // no, x1 // no
    for copy in second_copies:
        copy.wait_recv()
    total = sb2[lon].astype(F32)
    for k in range(1, no):
        total += rb2[k].astype(F32)
    sums_out[...] = total
    gain_row = jnp.broadcast_to(total[e2 + x2:e2 + x2 + 1], (8, C))
    gain_out[...] = pltpu.roll(gain_row, lax.rem(C - (lat * no + lon) * x2, C), 1)

    home.wait()
    for copy in back_copies:
        copy.wait_recv()
    for copy in x_copies + back_copies + hidden_copies + exit_copies + share_of_grad + tail_of_grad + second_copies:
        copy.wait_send()

    @pl.when(last)
    def _():
        for copy in c_copies:
            copy.wait_send()

    @pl.when(jnp.logical_not(first))
    def _():
        for copy in downs:
            copy.wait_send()


def call_kernel(sizes, names, args):
    ns, na, no = sizes
    e1, x1 = 3 * C // na, C // na
    e2, x2 = e1 // no, x1 // no
    r2 = round_up(e2 + x2 + 1, 16)
    spread = jnp.asarray(spread_table(), BF16)
    shares = jnp.asarray(share_table(e1, x1, 16, no, r2), BF16)
    hbm = pl.BlockSpec(memory_space=pltpu.HBM)
    vmem = pl.BlockSpec(memory_space=pltpu.VMEM)
    dma = pltpu.SemaphoreType.DMA
    n = LEVELS * GROUPS
    tile = (WLAT, WLON, LEVELS, C)
    parts = (4, WLAT // 2, WLON // 2, LEVELS, C)
    return pl.pallas_call(
        functools.partial(kernel, sizes, names),
        out_shape=(
            jax.ShapeDtypeStruct(tile, BF16),
            jax.ShapeDtypeStruct((r2, C), F32),
            jax.ShapeDtypeStruct((8, C), F32),
            jax.ShapeDtypeStruct((HEADS, RELPOS // 16), F32),
        ),
        in_specs=[hbm] * 8,
        out_specs=(hbm, vmem, vmem, vmem),
        scratch_shapes=[
            pltpu.VMEM(parts, BF16),
            pltpu.VMEM(parts, BF16),
            pltpu.VMEM((C, 3 * C), BF16),
            pltpu.VMEM((C, C), BF16),
            pltpu.VMEM((1, C), F32),
            pltpu.VMEM((HEADS, 1, RELPOS), F32),
            pltpu.VMEM(spread.shape, BF16),
            pltpu.VMEM(shares.shape, BF16),
            pltpu.VMEM((PAIRS, LANES), F32),
            pltpu.VMEM((PAIRS, LANES), F32),
            pltpu.VMEM((ROWS, LANES), F32),
            pltpu.VMEM((GROUPS, WIN, LANES), F32),
            pltpu.VMEM((WIN, C), F32),
            pltpu.VMEM((WIN, C), F32),
            pltpu.VMEM((ROWS, LANES), F32),
            pltpu.VMEM((n, LANES, STACK), BF16),
            pltpu.VMEM((n, STACK, LANES), BF16),
            pltpu.VMEM((n, LANES, LANES), BF16),
            pltpu.VMEM((n, LANES, LANES), BF16),
            pltpu.VMEM((ROWS, LANES), F32),
            pltpu.VMEM((WIN, C), F32),
            pltpu.VMEM((ROWS, LANES), F32),
            pltpu.VMEM((WIN, 3 * C), F32),
            pltpu.VMEM((WIN, C), F32),
            pltpu.VMEM((LEVELS, TOK + 8, C), BF16),
            pltpu.VMEM((LEVELS, TOK + 8, C), BF16),
            pltpu.VMEM(parts, BF16),
            pltpu.VMEM((WIN, C), BF16),
            pltpu.VMEM((na, WIN, C), BF16),
            pltpu.VMEM((na, x1, C), BF16),
            pltpu.VMEM((na, x1, C), BF16),
            pltpu.VMEM((na, WIN + 16, e1 - e1 % LANES), BF16),
            pltpu.VMEM((na, WIN + 16, e1 - e1 % LANES), BF16),
            pltpu.VMEM((na, e1 % LANES, 2 * LANES), BF16),
            pltpu.VMEM((na, e1 % LANES, 2 * LANES), BF16),
            pltpu.VMEM((no, r2, C), BF16),
            pltpu.VMEM((no, r2, C), BF16),
            pltpu.VMEM((8, 16, 2 * LANES), BF16),
            pltpu.VMEM((16, 16, 2 * LANES), BF16),
            dma((9,)), dma((4,)), dma((4,)), dma((4,)), dma((4,)), dma((2,)), dma((2,)), dma((4,)), dma((4,)),
            dma((na,)), dma((na,)), dma((na,)), dma((na,)), dma((na,)), dma((na,)), dma((na,)), dma((na,)), dma((no,)), dma((no,)), dma((8,)), dma((16,)),
        ],
        compiler_params=pltpu.CompilerParams(collective_id=0, has_side_effects=True, vmem_limit_bytes=56 * 2**20),
    )(*args, spread, shares)


def finish(share, ig_in, sums_in, gain_in, bias_in, ig_out, entry_out, exit_out, gain_out, bias_out):
    ig_out[...] = ig_in[...]
    entry_out[:, 0, :] = sums_in[0:3 * share]
    exit_out[:, 0, :] = sums_in[3 * share:4 * share]
    gain_out[...] = gain_in[0:1, 0:share]
    bias_out[:, 0, :] = bias_in[...]


def call_finish(share, *results):
    vmem = pl.BlockSpec(memory_space=pltpu.VMEM)
    return pl.pallas_call(
        functools.partial(finish, share),
        out_shape=(
            jax.ShapeDtypeStruct(results[0].shape, BF16),
            jax.ShapeDtypeStruct((3 * share, 1, C), F32),
            jax.ShapeDtypeStruct((share, 1, C), F32),
            jax.ShapeDtypeStruct((1, share), F32),
            jax.ShapeDtypeStruct((HEADS, 1, RELPOS // 16), F32),
        ),
        in_specs=[vmem] * 4,
        out_specs=(vmem,) * 5,
    )(*results)


def per_device(sizes, names, block_inputs, cotangent, input_projection, output_projection, norm_gain, earth_bias):
    ns, na, no = sizes
    args = (
        block_inputs[0].transpose(1, 2, 0, 3), cotangent.transpose(1, 2, 0, 3), input_projection, output_projection,
        norm_gain, earth_bias[0, 0, 0][:, None],
    )
    input_grad, sums, gain, bias = call_kernel(sizes, names, args)
    input_grad, entry, exits, gain, bias = call_finish(C // (na * no), input_grad, sums, gain, bias)
    return (
        input_grad.transpose(2, 0, 1, 3)[None], entry.transpose(1, 2, 0), exits.transpose(1, 2, 0), gain,
        bias[None, None].transpose(0, 1, 3, 2, 4),
    )


def solution(mesh):
    names = ("section", "lat", "lon")
    sizes = tuple(mesh.shape[name] for name in names)
    in_specs = (
        P("section", None, "lat", "lon", None),
        P(None, "lat", "lon", None),
        P("section", None, None),
        P("section", None, None),
        P("section", None),
        P("section", None, "lat", None, None),
    )
    out_specs = (
        P("section", None, "lat", "lon", None),
        P("section", None, ("lat", "lon")),
        P("section", None, ("lat", "lon")),
        P("section", ("lat", "lon")),
        P("section", None, "lat", None, "lon"),
    )
    return jax.shard_map(
        functools.partial(per_device, sizes, names), mesh=mesh, in_specs=in_specs, out_specs=out_specs, check_vma=False
    )
```

```python
import functools

import jax
import jax.numpy as jnp
import numpy as np
from jax import lax
from jax.experimental import pallas as pl
from jax.experimental.pallas import tpu as pltpu
from jax.sharding import PartitionSpec as P

MESH = pl.DeviceIdType.MESH
F32 = jnp.float32
BF16 = jnp.bfloat16

C = 384
HEADS = 12
HEAD_DIM = 32
WLAT = 6
WLON = 12
LEVELS = 2
TOK = WLAT * WLON
WIN = LEVELS * TOK
SPAN = 2 * WLON - 1
RELPOS = 3312
LANES = 128
GROUPS = C // LANES
PER_GROUP = LANES // HEAD_DIM
STACK = PER_GROUP * TOK
ROWS = LEVELS * HEADS * TOK
PAIRS = LEVELS * HEADS * WLAT
EPS = 1e-05
SCALE = HEAD_DIM ** -0.5
OFF = -1e30
BIAS_ROWS = (0, 1, 3, 4)


def round_up(n, m):
    return (n + m - 1) // m * m


def spread_table():
    out = np.zeros((2 * LANES, WLON, LANES), np.float32)
    for lq in range(WLON):
        for ak in range(WLAT):
            for lk in range(WLON):
                out[ak * SPAN + lq - lk + WLON - 1, lq, ak * WLON + lk] = 1.0
    return out.reshape(2 * LANES, WLON * LANES)


def share_table(entry, exits, gains, parts, rows):
    out = np.zeros((parts, rows, entry + exits + gains), np.float32)
    e, x = entry // parts, exits // parts
    for j in range(parts):
        for r in range(e):
            out[j, r, j * e + r] = 1.0
        for r in range(x):
            out[j, e + r, entry + j * x + r] = 1.0
        out[j, e + x, entry + exits] = 1.0
    return out.reshape(parts * rows, -1)


def dot(a, b):
    return jnp.dot(a, b, preferred_element_type=F32)


def dot_t(a, b):
    return lax.dot_general(a, b, (((1,), (1,)), ((), ())), preferred_element_type=F32)


def t_dot(a, b):
    return lax.dot_general(a, b, (((0,), (0,)), ((), ())), preferred_element_type=F32)


def kernel(
    sizes, names,
    x_hbm, ct_hbm, wi_hbm, wo_hbm, gain_hbm, tab_hbm, s_hbm, p2_hbm,
    ig_out, sums_out, gain_out, bias_out,
    xin, cin, wi_v, wo_v, wi_t, wo_t, gain_v, tab_v, s_v, p2_v, t0, t1, bias, wide, xs, gs, att, att_t, qm, kp, vp, mixes, mix, ds, pg,
    hg, gsend, grecv, rb, hs, hr, es, er, ms, mr, ts, tr, sb2, rb2, bsb, brb,
    load_sem, xsend_sem, xrecv_sem, csend_sem, crecv_sem, gsend_sem, grecv_sem, bksend_sem, bkrecv_sem,
    hsend_sem, hrecv_sem, esend_sem, erecv_sem, msend_sem, mrecv_sem, tsend_sem, trecv_sem, s2send, s2recv, bsend_sem, brecv_sem,
):
    ns, na, no = sizes
    nx = na // 2
    sec, lat, lon = (lax.axis_index(name) for name in names)
    n_sec, n_lat, n_lon = names
    lat_x, lat_y = lat // 2, lax.rem(lat, 2)

    def at_lat(k):
        return lax.rem(lat + k + na, na)

    def at_lon(k):
        return lax.rem(lon + k + no, no)

    def across(step):
        return lax.rem(lat_x + step[0], nx) * 2 + lax.rem(lat_y + step[1], 2)

    def slot(step):
        return 2 * step[0] + step[1]

    first, last = sec == 0, sec == ns - 1
    steps = [(dx, dy) for dx in range(nx) for dy in range(2) if dx or dy]
    steps.sort(key=lambda step: -(2 * min(step[0], nx - step[0]) + step[1]))
    turns = sorted(range(1, no), key=lambda k: -min(k, no - k))

    barrier = pltpu.get_barrier_semaphore()
    greeted = [{n_lon: at_lon(k)} for k in turns] + [{n_lat: across(step)} for step in steps]
    greeted += [{n_lat: at_lat(k), n_lon: at_lon(k)} for k in (-1, 1)]
    for device in greeted:
        pl.semaphore_signal(barrier, inc=1, device_id=device, device_id_type=MESH)

    @pl.when(jnp.logical_not(first))
    def _():
        pl.semaphore_signal(barrier, inc=1, device_id={n_sec: sec - 1}, device_id_type=MESH)

    @pl.when(jnp.logical_not(last))
    def _():
        pl.semaphore_signal(barrier, inc=1, device_id={n_sec: sec + 1}, device_id_type=MESH)

    halves = (pl.ds(3, 3), pl.ds(0, 3)), (pl.ds(6, 6), pl.ds(0, 6))
    quarters = ((0, 0), (0, 1), (1, 0), (1, 1))

    def quarter(ref, i):
        return ref.at[halves[0][quarters[i][0]], halves[1][quarters[i][1]]]

    loads = [
        (tab_hbm, tab_v), (s_hbm, s_v), (quarter(x_hbm, 0), xin.at[0]), (gain_hbm, gain_v),
        (wi_hbm.at[0], wi_v), (wo_hbm.at[0], wo_v), (p2_hbm, p2_v), (quarter(ct_hbm, 0), cin.at[0]),
    ]
    loads = [pltpu.make_async_copy(src, dst, load_sem.at[i]) for i, (src, dst) in enumerate(loads)]
    for copy in loads:
        copy.start()

    loads[0].wait()
    width = WLAT * SPAN
    for z in range(LEVELS):
        for a in range(WLAT):
            start = (z * 3 * WLAT + a) * width
            rows = pl.ds(z * HEADS * WLAT + a, HEADS, stride=WLAT)
            t0[rows, :] = tab_v[:, 0, start:start + LANES]
            rest = tab_v[:, 0, start + LANES:start + width]
            t1[rows, :] = jnp.concatenate([rest, jnp.zeros((HEADS, 2 * LANES - width), F32)], axis=1)
    table = jnp.concatenate([t0[...], t1[...]], axis=1)
    table_high = table.astype(BF16)
    table_low = (table - table_high.astype(F32)).astype(BF16)
    query_row = lax.rem(lax.broadcasted_iota(jnp.int32, (PAIRS, LANES), 0), WLAT)
    key = lax.broadcasted_iota(jnp.int32, (PAIRS, LANES), 1)
    apart = jnp.logical_and((query_row < 3) != (key < TOK // 2), lat == na - 1)
    closed = jnp.where(jnp.logical_or(apart, key >= TOK), OFF, 0.0)
    closed = jnp.concatenate([closed, closed], axis=1)
    loads[1].wait()
    for i in range(WLON // 2):
        spread = s_v[:, 2 * i * LANES:(2 * i + 2) * LANES]
        part = dot(table_high, spread) + dot(table_low, spread) + closed
        bias[pl.ds(2 * i, PAIRS, stride=WLON), :] = part[:, :LANES]
        bias[pl.ds(2 * i + 1, PAIRS, stride=WLON), :] = part[:, LANES:]

    loads[4].wait()
    loads[5].wait()
    wi_t[...] = wi_v[...].T
    wo_t[...] = wo_v[...].T
    pl.semaphore_wait(barrier, len(greeted) + jnp.minimum(sec, 1) + jnp.minimum(ns - 1 - sec, 1))

    def towards(i, sign):
        a, l = quarters[i]
        return ({n_lat: at_lat(sign)} if a else {}) | ({n_lon: at_lon(sign)} if l else {})

    def roll_copies(src, buffers, send, recv):
        return [
            pltpu.make_async_remote_copy(
                src_ref=quarter(src, i), dst_ref=buffers.at[i], send_sem=send.at[i], recv_sem=recv.at[i],
                device_id=towards(i, -1), device_id_type=MESH,
            )
            for i in (3, 2, 1)
        ]

    x_copies = roll_copies(x_hbm, xin, xsend_sem, xrecv_sem)
    for copy in x_copies:
        copy.start()
    c_copies = roll_copies(ct_hbm, cin, csend_sem, crecv_sem)

    @pl.when(last)
    def _():
        for copy in c_copies:
            copy.start()

    def assemble(buffers, out):
        for i, (a, l) in enumerate(quarters):
            for r in range(3):
                row = ((3 * a + r) * WLON + 6 * l) * LEVELS
                for b in range(GROUPS):
                    part = buffers[i, r, :, :, b * LANES:(b + 1) * LANES].astype(F32)
                    wide[b, row:row + 6 * LEVELS, :] = part.reshape(6 * LEVELS, LANES)
        for z in range(LEVELS):
            for b in range(GROUPS):
                rows = pl.ds(1 - z, TOK, stride=LEVELS)
                out[z * TOK:(z + 1) * TOK, b * LANES:(b + 1) * LANES] = wide[b, rows, :]

    loads[2].wait()
    for copy in x_copies:
        copy.wait_recv()
    assemble(xin, xs)
    x = xs[...]
    centered = x - jnp.mean(x, axis=-1, keepdims=True)
    inverse = lax.rsqrt(jnp.mean(centered * centered, axis=-1, keepdims=True) + EPS)
    normed = centered * inverse
    loads[3].wait()
    gain = gain_v[...]
    hidden = (normed * gain).astype(BF16)
    hs[...] = hidden

    def share_copies(src, dst, send, recv):
        return [
            pltpu.make_async_remote_copy(
                src_ref=src.at[across(step)], dst_ref=dst.at[slot(step)],
                send_sem=send.at[slot(step)], recv_sem=recv.at[slot(step)],
                device_id={n_lat: across(step)}, device_id_type=MESH,
            )
            for step in steps
        ]

    hidden_copies = []
    for step in steps:
        through = step[0] and step[1]
        hidden_copies.append(pltpu.make_async_remote_copy(
            src_ref=hr.at[1] if through else hs, dst_ref=hr.at[slot(step)],
            send_sem=hsend_sem.at[slot(step)], recv_sem=hrecv_sem.at[slot(step)],
            device_id={n_lat: across((step[0], 0) if through else step)}, device_id_type=MESH,
        ))
    hidden_copies[steps.index((0, 1))].start()

    def pass_hidden():
        hidden_copies[steps.index((0, 1))].wait_recv()
        for step, copy in zip(steps, hidden_copies):
            if step[0]:
                copy.start()

    projected = dot(hidden, wi_v[...]).astype(BF16).astype(F32)

    head_of_lane = lax.broadcasted_iota(jnp.int32, (TOK, LANES), 1) // HEAD_DIM

    def stack_heads(part):
        return jnp.concatenate([jnp.where(head_of_lane == h, part, 0.0) for h in range(PER_GROUP)], axis=0)

    def unstack_heads(stacked):
        total = jnp.where(head_of_lane == 0, stacked[0:TOK], 0.0)
        for h in range(1, PER_GROUP):
            total = jnp.where(head_of_lane == h, stacked[h * TOK:(h + 1) * TOK], total)
        return total

    def pad_keys(part):
        return jnp.concatenate([part, jnp.zeros((LANES - TOK, LANES), F32)], axis=0).astype(BF16)

    def place(z, g):
        i = z * GROUPS + g
        return i, slice(z * TOK, (z + 1) * TOK), slice(g * LANES, (g + 1) * LANES), slice(i * STACK, (i + 1) * STACK)

    places = [(z, g) for z in range(LEVELS) for g in range(GROUPS)]
    for z, g in places:
        i, tokens, lanes, stacked_rows = place(z, g)
        queries = stack_heads(projected[tokens, g * LANES:(g + 1) * LANES]).astype(BF16)
        keys = pad_keys(projected[tokens, C + g * LANES:C + (g + 1) * LANES])
        values = pad_keys(projected[tokens, 2 * C + g * LANES:2 * C + (g + 1) * LANES])
        qm[i] = queries
        kp[i] = keys
        vp[i] = jnp.concatenate([values.T, jnp.full((LANES, LANES), -1.0, BF16)], axis=0)
        raised = jnp.exp(dot_t(queries, keys) * SCALE + bias[stacked_rows, :])
        attention = raised / jnp.sum(raised, axis=-1, keepdims=True)
        att[stacked_rows, :] = attention
        att_t[i] = attention.T.astype(BF16)
        mixed = dot(attention.astype(BF16), values)
        mixes[stacked_rows, :] = mixed
        mix[tokens, lanes] = unstack_heads(mixed)
    pass_hidden()

    loads[7].wait()

    @pl.when(last)
    def _():
        for copy in c_copies:
            copy.wait_recv()
        assemble(cin, gs)


    downs = [
        pltpu.make_async_remote_copy(
            src_ref=gsend.at[z], dst_ref=grecv.at[z], send_sem=gsend_sem.at[z], recv_sem=grecv_sem.at[z],
            device_id={n_sec: jnp.maximum(sec - 1, 0)}, device_id_type=MESH,
        )
        for z in range(LEVELS)
    ]
    e1, x1 = 3 * C // na, C // na
    rest = e1 % LANES
    exit_copies = share_copies(es, er, esend_sem, erecv_sem)

    def send_exits():
        exits = t_dot(gs[...].astype(BF16), mix[...].astype(BF16)).astype(BF16)
        for i in range(na):
            es[i] = exits[i * x1:(i + 1) * x1]
        for copy in exit_copies:
            copy.start()

    for z in range(LEVELS):
        tokens = slice(z * TOK, (z + 1) * TOK)

        @pl.when(jnp.logical_not(last))
        def _(z=z, tokens=tokens):
            downs[z].wait_recv()
            gs[tokens, :] = grecv[z].astype(F32)[:TOK]

        if z == LEVELS - 1:
            pl.when(sec < ns // 2)(send_exits)
        grad = gs[tokens, :]
        mixed_grad = dot(grad.astype(BF16), wo_t[...]).astype(BF16).astype(F32)
        for g in range(GROUPS):
            i, _, lanes, stacked_rows = place(z, g)
            outer = stack_heads(mixed_grad[:, lanes])
            both = jnp.concatenate([outer, outer * mixes[stacked_rows, :]], axis=1).astype(BF16)
            outer = outer.astype(BF16)
            score = att[stacked_rows, :] * dot(both, vp[i])
            ds[stacked_rows, :] = score
            score_low = score.astype(BF16)
            pg[tokens, g * LANES:(g + 1) * LANES] = unstack_heads(dot(score_low, kp[i])) * SCALE
            pg[tokens, C + g * LANES:C + (g + 1) * LANES] = t_dot(score_low, qm[i])[:TOK] * SCALE
            pg[tokens, 2 * C + g * LANES:2 * C + (g + 1) * LANES] = dot(att_t[i], outer)[:TOK]
        hidden_grad = dot(pg[tokens, :].astype(BF16), wi_t[...]).astype(BF16).astype(F32)
        hg[tokens, :] = hidden_grad
        normed_grad = hidden_grad * gain
        mine = normed[tokens]
        along = jnp.mean(normed_grad * mine, axis=-1, keepdims=True)
        inner = normed_grad - jnp.mean(normed_grad, axis=-1, keepdims=True) - mine * along
        input_grad = grad + inverse[tokens] * inner
        gsend[z] = jnp.concatenate([input_grad, jnp.zeros((8, C), F32)], axis=0).astype(BF16)

        @pl.when(jnp.logical_not(first))
        def _(z=z):
            downs[z].start()

        for b in range(GROUPS):
            wide[b, pl.ds(1 - z, TOK, stride=LEVELS), :] = input_grad[:, b * LANES:(b + 1) * LANES]

    wide_share = ms.shape[2]
    gain_grad = jnp.sum(hg[...] * normed, axis=0, keepdims=True)
    spare = round_up(C, wide_share) - C
    if spare:
        gain_grad = jnp.concatenate([gain_grad, jnp.zeros((1, spare), F32)], axis=1)
    gain_parts = [gain_grad[:, at:at + wide_share] for at in range(0, C, wide_share)]
    gain_rows = jnp.concatenate(gain_parts + [jnp.zeros((16 - len(gain_parts), wide_share), F32)], axis=0).astype(BF16)
    tails = [pg[:, (i + 1) * e1 - rest:(i + 1) * e1] for i in range(na)]
    tails = jnp.concatenate(tails, axis=1).T
    tails = jnp.concatenate([tails, jnp.zeros((na * rest, 2 * LANES - WIN), F32)], axis=1).astype(BF16)
    for i in range(na):
        ms[i, 0:WIN, :] = pg[:, i * e1:(i + 1) * e1 - rest].astype(BF16)
        ms[i, WIN:WIN + 16, :] = gain_rows
        ts[i] = tails[i * rest:(i + 1) * rest]
    share_of_grad = share_copies(ms, mr, msend_sem, mrecv_sem)
    tail_of_grad = share_copies(ts, tr, tsend_sem, trecv_sem)
    for copy, tail_copy in zip(share_of_grad, tail_of_grad):
        copy.start()
        tail_copy.start()
    pl.when(sec >= ns // 2)(send_exits)

    for i, (a, l) in enumerate(quarters):
        for r in range(3):
            row = ((3 * a + r) * WLON + 6 * l) * LEVELS
            for b in range(GROUPS):
                part = wide[b, row:row + 6 * LEVELS, :].reshape(6, LEVELS, LANES)
                rb[i, r, :, :, b * LANES:(b + 1) * LANES] = part.astype(BF16)
    home = pltpu.make_async_copy(rb.at[0], quarter(ig_out, 0), load_sem.at[8])
    home.start()
    back_copies = [
        pltpu.make_async_remote_copy(
            src_ref=rb.at[i], dst_ref=quarter(ig_out, i), send_sem=bksend_sem.at[i], recv_sem=bkrecv_sem.at[i],
            device_id=towards(i, 1), device_id_type=MESH,
        )
        for i in (3, 2, 1)
    ]
    for copy in back_copies:
        copy.start()

    folded = jnp.zeros((PAIRS, 2 * LANES), F32)
    for lq in range(WLON):
        part = ds[pl.ds(lq, PAIRS, stride=WLON), :].astype(BF16)
        folded += dot_t(part, s_v[:, lq * LANES:(lq + 1) * LANES])
    t0[...] = folded[:, :LANES]
    t1[...] = folded[:, LANES:]
    for u in range(8):
        upper, lower = (
            jnp.concatenate([t0[rows, :], t1[rows, :]], axis=1)
            for rows in (pl.ds(u // 4 * HEADS * WLAT + BIAS_ROWS[u % 4] + k, HEADS, stride=WLAT) for k in range(2))
        )
        half = width // 2
        if u % 2 == 0:
            lower = lower[:, :half]
        else:
            upper, lower = upper[:, half:width], lower[:, :width]
        both = jnp.concatenate([upper[:, :width], lower, jnp.zeros((HEADS, 2 * LANES - RELPOS // 16), F32)], axis=1)
        bsb[u] = jnp.concatenate([both, jnp.zeros((16 - HEADS, 2 * LANES), F32)], axis=0).astype(BF16)
    if no == 16:
        def bias_copy(u, k):
            target = u if u < 4 else u + 8
            return target, pltpu.make_async_remote_copy(
                src_ref=bsb.at[u], dst_ref=brb.at[k], send_sem=bsend_sem.at[u], recv_sem=brecv_sem.at[k],
                device_id={n_lon: jnp.int32(target)}, device_id_type=MESH,
            )

        for u in range(8):
            target, copy = bias_copy(u, lon)

            @pl.when(lon != target)
            def _(copy=copy):
                copy.start()

    loads[6].wait()
    own = ms[lat]
    entry = t_dot(own[:WIN], hidden)
    entry_tail = dot(ts[lat][:, :WIN], hidden)
    exits = es[lat].astype(F32)
    gain_total = own[WIN:WIN + 16].astype(F32)
    for i in reversed(range(len(steps))):
        k = slot(steps[i])
        if steps[i] != (0, 1):
            hidden_copies[i].wait_recv()
        for copies in (exit_copies, share_of_grad, tail_of_grad):
            copies[i].wait_recv()
        entry += t_dot(mr[k][:WIN], hr[k])
        entry_tail += dot(tr[k][:, :WIN], hr[k])
        exits += er[k].astype(F32)
        gain_total += mr[k][WIN:WIN + 16].astype(F32)
    gain_total = jnp.concatenate([gain_total[i:i + 1] for i in range(len(gain_parts))], axis=1)[:, :C]
    total = jnp.concatenate([entry, entry_tail, exits, gain_total, jnp.zeros((15, C), F32)], axis=0)
    sb2[...] = dot(p2_v[...], total.astype(BF16)).astype(BF16).reshape(sb2.shape)
    second_copies = [
        pltpu.make_async_remote_copy(
            src_ref=sb2.at[at_lon(k)], dst_ref=rb2.at[k], send_sem=s2send.at[k], recv_sem=s2recv.at[k],
            device_id={n_lon: at_lon(k)}, device_id_type=MESH,
        )
        for k in turns
    ]
    for copy in second_copies:
        copy.start()

    if no == 16:
        keeps = jnp.logical_or(lon < 4, lon >= 12)
        bias_out[...] = jnp.zeros_like(bias_out)

        @pl.when(keeps)
        def _():
            for s in range(no):
                @pl.when(lon != s)
                def _():
                    bias_copy(0, s)[1].wait_recv()
            brb[lon] = bsb[jnp.where(lon < 4, lon, lon - 8)]
            total = brb[0].astype(F32)
            for s in range(1, no):
                total += brb[s].astype(F32)
            bias_out[...] = total[:HEADS, :RELPOS // 16]

        for u in range(8):
            target, copy = bias_copy(u, lon)

            @pl.when(lon != target)
            def _(copy=copy):
                copy.wait_send()
    else:
        bias_out[...] = jnp.zeros_like(bias_out)

    e2, x2 = e1 // no, x1 // no
    for copy in second_copies:
        copy.wait_recv()
    total = sb2[lon].astype(F32)
    for k in range(1, no):
        total += rb2[k].astype(F32)
    sums_out[...] = total
    gain_row = jnp.broadcast_to(total[e2 + x2:e2 + x2 + 1], (8, C))
    gain_out[...] = pltpu.roll(gain_row, lax.rem(C - (lat * no + lon) * x2, C), 1)

    home.wait()
    for copy in back_copies:
        copy.wait_recv()
    for copy in x_copies + back_copies + hidden_copies + exit_copies + share_of_grad + tail_of_grad + second_copies:
        copy.wait_send()

    @pl.when(last)
    def _():
        for copy in c_copies:
            copy.wait_send()

    @pl.when(jnp.logical_not(first))
    def _():
        for copy in downs:
            copy.wait_send()


def call_kernel(sizes, names, args):
    ns, na, no = sizes
    e1, x1 = 3 * C // na, C // na
    e2, x2 = e1 // no, x1 // no
    r2 = round_up(e2 + x2 + 1, 16)
    spread = jnp.asarray(spread_table(), BF16)
    shares = jnp.asarray(share_table(e1, x1, 16, no, r2), BF16)
    hbm = pl.BlockSpec(memory_space=pltpu.HBM)
    vmem = pl.BlockSpec(memory_space=pltpu.VMEM)
    dma = pltpu.SemaphoreType.DMA
    n = LEVELS * GROUPS
    tile = (WLAT, WLON, LEVELS, C)
    parts = (4, WLAT // 2, WLON // 2, LEVELS, C)
    return pl.pallas_call(
        functools.partial(kernel, sizes, names),
        out_shape=(
            jax.ShapeDtypeStruct(tile, BF16),
            jax.ShapeDtypeStruct((r2, C), F32),
            jax.ShapeDtypeStruct((8, C), F32),
            jax.ShapeDtypeStruct((HEADS, RELPOS // 16), F32),
        ),
        in_specs=[hbm] * 8,
        out_specs=(hbm, vmem, vmem, vmem),
        scratch_shapes=[
            pltpu.VMEM(parts, BF16),
            pltpu.VMEM(parts, BF16),
            pltpu.VMEM((C, 3 * C), BF16),
            pltpu.VMEM((C, C), BF16),
            pltpu.VMEM((3 * C, C), BF16),
            pltpu.VMEM((C, C), BF16),
            pltpu.VMEM((1, C), F32),
            pltpu.VMEM((HEADS, 1, RELPOS), F32),
            pltpu.VMEM(spread.shape, BF16),
            pltpu.VMEM(shares.shape, BF16),
            pltpu.VMEM((PAIRS, LANES), F32),
            pltpu.VMEM((PAIRS, LANES), F32),
            pltpu.VMEM((ROWS, LANES), F32),
            pltpu.VMEM((GROUPS, WIN, LANES), F32),
            pltpu.VMEM((WIN, C), F32),
            pltpu.VMEM((WIN, C), F32),
            pltpu.VMEM((ROWS, LANES), F32),
            pltpu.VMEM((n, LANES, STACK), BF16),
            pltpu.VMEM((n, STACK, LANES), BF16),
            pltpu.VMEM((n, LANES, LANES), BF16),
            pltpu.VMEM((n, 2 * LANES, LANES), BF16),
            pltpu.VMEM((ROWS, LANES), F32),
            pltpu.VMEM((WIN, C), F32),
            pltpu.VMEM((ROWS, LANES), F32),
            pltpu.VMEM((WIN, 3 * C), F32),
            pltpu.VMEM((WIN, C), F32),
            pltpu.VMEM((LEVELS, TOK + 8, C), BF16),
            pltpu.VMEM((LEVELS, TOK + 8, C), BF16),
            pltpu.VMEM(parts, BF16),
            pltpu.VMEM((WIN, C), BF16),
            pltpu.VMEM((na, WIN, C), BF16),
            pltpu.VMEM((na, x1, C), BF16),
            pltpu.VMEM((na, x1, C), BF16),
            pltpu.VMEM((na, WIN + 16, e1 - e1 % LANES), BF16),
            pltpu.VMEM((na, WIN + 16, e1 - e1 % LANES), BF16),
            pltpu.VMEM((na, e1 % LANES, 2 * LANES), BF16),
            pltpu.VMEM((na, e1 % LANES, 2 * LANES), BF16),
            pltpu.VMEM((no, r2, C), BF16),
            pltpu.VMEM((no, r2, C), BF16),
            pltpu.VMEM((8, 16, 2 * LANES), BF16),
            pltpu.VMEM((16, 16, 2 * LANES), BF16),
            dma((9,)), dma((4,)), dma((4,)), dma((4,)), dma((4,)), dma((2,)), dma((2,)), dma((4,)), dma((4,)),
            dma((na,)), dma((na,)), dma((na,)), dma((na,)), dma((na,)), dma((na,)), dma((na,)), dma((na,)), dma((no,)), dma((no,)), dma((8,)), dma((16,)),
        ],
        compiler_params=pltpu.CompilerParams(collective_id=0, has_side_effects=True, vmem_limit_bytes=56 * 2**20),
    )(*args, spread, shares)


def finish(share, ig_in, sums_in, gain_in, bias_in, ig_out, entry_out, exit_out, gain_out, bias_out):
    ig_out[...] = ig_in[...]
    entry_out[:, 0, :] = sums_in[0:3 * share]
    exit_out[:, 0, :] = sums_in[3 * share:4 * share]
    gain_out[...] = gain_in[0:1, 0:share]
    bias_out[:, 0, :] = bias_in[...]


def call_finish(share, *results):
    vmem = pl.BlockSpec(memory_space=pltpu.VMEM)
    return pl.pallas_call(
        functools.partial(finish, share),
        out_shape=(
            jax.ShapeDtypeStruct(results[0].shape, BF16),
            jax.ShapeDtypeStruct((3 * share, 1, C), F32),
            jax.ShapeDtypeStruct((share, 1, C), F32),
            jax.ShapeDtypeStruct((1, share), F32),
            jax.ShapeDtypeStruct((HEADS, 1, RELPOS // 16), F32),
        ),
        in_specs=[vmem] * 4,
        out_specs=(vmem,) * 5,
    )(*results)


def per_device(sizes, names, block_inputs, cotangent, input_projection, output_projection, norm_gain, earth_bias):
    ns, na, no = sizes
    args = (
        block_inputs[0].transpose(1, 2, 0, 3), cotangent.transpose(1, 2, 0, 3), input_projection, output_projection,
        norm_gain, earth_bias[0, 0, 0][:, None],
    )
    input_grad, sums, gain, bias = call_kernel(sizes, names, args)
    input_grad, entry, exits, gain, bias = call_finish(C // (na * no), input_grad, sums, gain, bias)
    return (
        input_grad.transpose(2, 0, 1, 3)[None], entry.transpose(1, 2, 0), exits.transpose(1, 2, 0), gain,
        bias[None, None].transpose(0, 1, 3, 2, 4),
    )


def solution(mesh):
    names = ("section", "lat", "lon")
    sizes = tuple(mesh.shape[name] for name in names)
    in_specs = (
        P("section", None, "lat", "lon", None),
        P(None, "lat", "lon", None),
        P("section", None, None),
        P("section", None, None),
        P("section", None),
        P("section", None, "lat", None, None),
    )
    out_specs = (
        P("section", None, "lat", "lon", None),
        P("section", None, ("lat", "lon")),
        P("section", None, ("lat", "lon")),
        P("section", ("lat", "lon")),
        P("section", None, "lat", None, "lon"),
    )
    return jax.shard_map(
        functools.partial(per_device, sizes, names), mesh=mesh, in_specs=in_specs, out_specs=out_specs, check_vma=False
    )
```

```python
import functools

import jax
import jax.numpy as jnp
import numpy as np
from jax import lax
from jax.experimental import pallas as pl
from jax.experimental.pallas import tpu as pltpu
from jax.sharding import PartitionSpec as P

MESH = pl.DeviceIdType.MESH
F32 = jnp.float32
BF16 = jnp.bfloat16

C = 384
HEADS = 12
HEAD_DIM = 32
WLAT = 6
WLON = 12
LEVELS = 2
TOK = WLAT * WLON
WIN = LEVELS * TOK
SPAN = 2 * WLON - 1
RELPOS = 3312
LANES = 128
GROUPS = C // LANES
PER_GROUP = LANES // HEAD_DIM
STACK = PER_GROUP * TOK
ROWS = LEVELS * HEADS * TOK
PAIRS = LEVELS * HEADS * WLAT
EPS = 1e-05
SCALE = HEAD_DIM ** -0.5
OFF = -1e30
BIAS_ROWS = (0, 1, 3, 4)


def round_up(n, m):
    return (n + m - 1) // m * m


def spread_table():
    out = np.zeros((2 * LANES, WLON, LANES), np.float32)
    for lq in range(WLON):
        for ak in range(WLAT):
            for lk in range(WLON):
                out[ak * SPAN + lq - lk + WLON - 1, lq, ak * WLON + lk] = 1.0
    return out.reshape(2 * LANES, WLON * LANES)


def share_table(entry, exits, gains, parts, rows):
    out = np.zeros((parts, rows, entry + exits + gains), np.float32)
    e, x = entry // parts, exits // parts
    for j in range(parts):
        for r in range(e):
            out[j, r, j * e + r] = 1.0
        for r in range(x):
            out[j, e + r, entry + j * x + r] = 1.0
        out[j, e + x, entry + exits] = 1.0
    return out.reshape(parts * rows, -1)


def dot(a, b):
    return jnp.dot(a, b, preferred_element_type=F32)


def dot_t(a, b):
    return lax.dot_general(a, b, (((1,), (1,)), ((), ())), preferred_element_type=F32)


def t_dot(a, b):
    return lax.dot_general(a, b, (((0,), (0,)), ((), ())), preferred_element_type=F32)


def kernel(
    sizes, names,
    x_hbm, ct_hbm, wi_hbm, wo_hbm, gain_hbm, tab_hbm, s_hbm, p2_hbm,
    ig_out, sums_out, gain_out, bias_out,
    xin, cin, wi_v, wo_v, wi_t, wo_t, gain_v, tab_v, s_v, p2_v, t0, t1, bias, wide, xs, gs, att, att_t, qm, kp, vp, mixes, mix, ds, pg,
    hg, gsend, grecv, rb, hs, hr, es, er, ms, mr, ts, tr, sb2, rb2, bsb, brb,
    load_sem, xsend_sem, xrecv_sem, csend_sem, crecv_sem, gsend_sem, grecv_sem, bksend_sem, bkrecv_sem,
    hsend_sem, hrecv_sem, esend_sem, erecv_sem, msend_sem, mrecv_sem, tsend_sem, trecv_sem, s2send, s2recv, bsend_sem, brecv_sem,
):
    ns, na, no = sizes
    nx = na // 2
    sec, lat, lon = (lax.axis_index(name) for name in names)
    n_sec, n_lat, n_lon = names
    lat_x, lat_y = lat // 2, lax.rem(lat, 2)

    def at_lat(k):
        return lax.rem(lat + k + na, na)

    def at_lon(k):
        return lax.rem(lon + k + no, no)

    def across(step):
        return lax.rem(lat_x + step[0], nx) * 2 + lax.rem(lat_y + step[1], 2)

    def slot(step):
        return 2 * step[0] + step[1]

    first, last = sec == 0, sec == ns - 1
    steps = [(dx, dy) for dx in range(nx) for dy in range(2) if dx or dy]
    steps.sort(key=lambda step: -(2 * min(step[0], nx - step[0]) + step[1]))
    turns = sorted(range(1, no), key=lambda k: -min(k, no - k))

    barrier = pltpu.get_barrier_semaphore()
    greeted = [{n_lon: at_lon(k)} for k in turns] + [{n_lat: across(step)} for step in steps]
    greeted += [{n_lat: at_lat(k), n_lon: at_lon(k)} for k in (-1, 1)]
    for device in greeted:
        pl.semaphore_signal(barrier, inc=1, device_id=device, device_id_type=MESH)

    @pl.when(jnp.logical_not(first))
    def _():
        pl.semaphore_signal(barrier, inc=1, device_id={n_sec: sec - 1}, device_id_type=MESH)

    @pl.when(jnp.logical_not(last))
    def _():
        pl.semaphore_signal(barrier, inc=1, device_id={n_sec: sec + 1}, device_id_type=MESH)

    halves = (pl.ds(3, 3), pl.ds(0, 3)), (pl.ds(6, 6), pl.ds(0, 6))
    quarters = ((0, 0), (0, 1), (1, 0), (1, 1))

    def quarter(ref, i):
        return ref.at[halves[0][quarters[i][0]], halves[1][quarters[i][1]]]

    loads = [
        (tab_hbm, tab_v), (s_hbm, s_v), (quarter(x_hbm, 0), xin.at[0]), (gain_hbm, gain_v),
        (wi_hbm.at[0], wi_v), (wo_hbm.at[0], wo_v), (p2_hbm, p2_v), (quarter(ct_hbm, 0), cin.at[0]),
    ]
    loads = [pltpu.make_async_copy(src, dst, load_sem.at[i]) for i, (src, dst) in enumerate(loads)]
    for copy in loads:
        copy.start()

    loads[0].wait()
    width = WLAT * SPAN
    for z in range(LEVELS):
        for a in range(WLAT):
            start = (z * 3 * WLAT + a) * width
            rows = pl.ds(z * HEADS * WLAT + a, HEADS, stride=WLAT)
            t0[rows, :] = tab_v[:, 0, start:start + LANES]
            rest = tab_v[:, 0, start + LANES:start + width]
            t1[rows, :] = jnp.concatenate([rest, jnp.zeros((HEADS, 2 * LANES - width), F32)], axis=1)
    table = jnp.concatenate([t0[...], t1[...]], axis=1)
    table_high = table.astype(BF16)
    table_low = (table - table_high.astype(F32)).astype(BF16)
    query_row = lax.rem(lax.broadcasted_iota(jnp.int32, (PAIRS, LANES), 0), WLAT)
    key = lax.broadcasted_iota(jnp.int32, (PAIRS, LANES), 1)
    apart = jnp.logical_and((query_row < 3) != (key < TOK // 2), lat == na - 1)
    closed = jnp.where(jnp.logical_or(apart, key >= TOK), OFF, 0.0)
    closed = jnp.concatenate([closed, closed], axis=1)
    loads[1].wait()
    for i in range(WLON // 2):
        spread = s_v[:, 2 * i * LANES:(2 * i + 2) * LANES]
        part = dot(table_high, spread) + dot(table_low, spread) + closed
        bias[pl.ds(2 * i, PAIRS, stride=WLON), :] = part[:, :LANES]
        bias[pl.ds(2 * i + 1, PAIRS, stride=WLON), :] = part[:, LANES:]

    loads[4].wait()
    loads[5].wait()
    wi_t[...] = wi_v[...].T
    wo_t[...] = wo_v[...].T
    pl.semaphore_wait(barrier, len(greeted) + jnp.minimum(sec, 1) + jnp.minimum(ns - 1 - sec, 1))

    def towards(i, sign):
        a, l = quarters[i]
        return ({n_lat: at_lat(sign)} if a else {}) | ({n_lon: at_lon(sign)} if l else {})

    def roll_copies(src, buffers, send, recv):
        return [
            pltpu.make_async_remote_copy(
                src_ref=quarter(src, i), dst_ref=buffers.at[i], send_sem=send.at[i], recv_sem=recv.at[i],
                device_id=towards(i, -1), device_id_type=MESH,
            )
            for i in (3, 2, 1)
        ]

    x_copies = roll_copies(x_hbm, xin, xsend_sem, xrecv_sem)
    for copy in x_copies:
        copy.start()
    c_copies = roll_copies(ct_hbm, cin, csend_sem, crecv_sem)

    @pl.when(last)
    def _():
        for copy in c_copies:
            copy.start()

    def assemble(buffers, out):
        for i, (a, l) in enumerate(quarters):
            for r in range(3):
                row = ((3 * a + r) * WLON + 6 * l) * LEVELS
                for b in range(GROUPS):
                    part = buffers[i, r, :, :, b * LANES:(b + 1) * LANES].astype(F32)
                    wide[b, row:row + 6 * LEVELS, :] = part.reshape(6 * LEVELS, LANES)
        for z in range(LEVELS):
            for b in range(GROUPS):
                rows = pl.ds(1 - z, TOK, stride=LEVELS)
                out[z * TOK:(z + 1) * TOK, b * LANES:(b + 1) * LANES] = wide[b, rows, :]

    loads[2].wait()
    for copy in x_copies:
        copy.wait_recv()
    assemble(xin, xs)
    x = xs[...]
    centered = x - jnp.mean(x, axis=-1, keepdims=True)
    inverse = lax.rsqrt(jnp.mean(centered * centered, axis=-1, keepdims=True) + EPS)
    normed = centered * inverse
    loads[3].wait()
    gain = gain_v[...]
    hidden = (normed * gain).astype(BF16)
    hs[...] = hidden

    def share_copies(src, dst, send, recv):
        return [
            pltpu.make_async_remote_copy(
                src_ref=src.at[across(step)], dst_ref=dst.at[slot(step)],
                send_sem=send.at[slot(step)], recv_sem=recv.at[slot(step)],
                device_id={n_lat: across(step)}, device_id_type=MESH,
            )
            for step in steps
        ]

    hidden_copies = []
    for step in steps:
        through = step[0] and step[1]
        hidden_copies.append(pltpu.make_async_remote_copy(
            src_ref=hr.at[1] if through else hs, dst_ref=hr.at[slot(step)],
            send_sem=hsend_sem.at[slot(step)], recv_sem=hrecv_sem.at[slot(step)],
            device_id={n_lat: across((step[0], 0) if through else step)}, device_id_type=MESH,
        ))
    hidden_copies[steps.index((0, 1))].start()

    def pass_hidden():
        hidden_copies[steps.index((0, 1))].wait_recv()
        for step, copy in zip(steps, hidden_copies):
            if step[0]:
                copy.start()

    projected = dot(hidden, wi_v[...]).astype(BF16).astype(F32)

    head_of_lane = lax.broadcasted_iota(jnp.int32, (TOK, LANES), 1) // HEAD_DIM

    def stack_heads(part):
        return jnp.concatenate([jnp.where(head_of_lane == h, part, 0.0) for h in range(PER_GROUP)], axis=0)

    def unstack_heads(stacked):
        total = jnp.where(head_of_lane == 0, stacked[0:TOK], 0.0)
        for h in range(1, PER_GROUP):
            total = jnp.where(head_of_lane == h, stacked[h * TOK:(h + 1) * TOK], total)
        return total

    def pad_keys(part):
        return jnp.concatenate([part, jnp.zeros((LANES - TOK, LANES), F32)], axis=0).astype(BF16)

    def place(z, g):
        i = z * GROUPS + g
        return i, slice(z * TOK, (z + 1) * TOK), slice(g * LANES, (g + 1) * LANES), slice(i * STACK, (i + 1) * STACK)

    places = [(z, g) for z in range(LEVELS) for g in range(GROUPS)]
    for z, g in places:
        i, tokens, lanes, stacked_rows = place(z, g)
        queries = stack_heads(projected[tokens, g * LANES:(g + 1) * LANES]).astype(BF16)
        keys = pad_keys(projected[tokens, C + g * LANES:C + (g + 1) * LANES])
        values = pad_keys(projected[tokens, 2 * C + g * LANES:2 * C + (g + 1) * LANES])
        qm[i] = queries
        kp[i] = keys
        vp[i] = jnp.concatenate([values.T, jnp.full((LANES, LANES), -1.0, BF16)], axis=0)
        raised = jnp.exp(dot_t(queries, keys) * SCALE + bias[stacked_rows, :])
        attention = raised / jnp.sum(raised, axis=-1, keepdims=True)
        att[stacked_rows, :] = attention
        att_t[i] = attention.T.astype(BF16)
        mixed = dot(attention.astype(BF16), values)
        mixes[stacked_rows, :] = mixed
        mix[tokens, lanes] = unstack_heads(mixed)
    pass_hidden()

    loads[7].wait()

    @pl.when(last)
    def _():
        for copy in c_copies:
            copy.wait_recv()
        assemble(cin, gs)


    downs = [
        pltpu.make_async_remote_copy(
            src_ref=gsend.at[z], dst_ref=grecv.at[z], send_sem=gsend_sem.at[z], recv_sem=grecv_sem.at[z],
            device_id={n_sec: jnp.maximum(sec - 1, 0)}, device_id_type=MESH,
        )
        for z in range(LEVELS)
    ]
    e1, x1 = 3 * C // na, C // na
    rest = e1 % LANES
    exit_copies = share_copies(es, er, esend_sem, erecv_sem)

    def send_exits():
        exits = t_dot(gs[...].astype(BF16), mix[...].astype(BF16)).astype(BF16)
        for i in range(na):
            es[i] = exits[i * x1:(i + 1) * x1]
        for copy in exit_copies:
            copy.start()

    for z in range(LEVELS):
        tokens = slice(z * TOK, (z + 1) * TOK)

        @pl.when(jnp.logical_not(last))
        def _(z=z, tokens=tokens):
            downs[z].wait_recv()
            gs[tokens, :] = grecv[z].astype(F32)[:TOK]

        if z == LEVELS - 1:
            pl.when(sec < ns // 2)(send_exits)
        grad = gs[tokens, :]
        mixed_grad = dot(grad.astype(BF16), wo_t[...]).astype(BF16).astype(F32)
        for g in range(GROUPS):
            i, _, lanes, stacked_rows = place(z, g)
            outer = stack_heads(mixed_grad[:, lanes])
            both = jnp.concatenate([outer, outer * mixes[stacked_rows, :]], axis=1).astype(BF16)
            outer = outer.astype(BF16)
            score = att[stacked_rows, :] * dot(both, vp[i])
            ds[stacked_rows, :] = score
            score_low = score.astype(BF16)
            pg[tokens, g * LANES:(g + 1) * LANES] = unstack_heads(dot(score_low, kp[i])) * SCALE
            pg[tokens, C + g * LANES:C + (g + 1) * LANES] = t_dot(score_low, qm[i])[:TOK] * SCALE
            pg[tokens, 2 * C + g * LANES:2 * C + (g + 1) * LANES] = dot(att_t[i], outer)[:TOK]
        hidden_grad = dot(pg[tokens, :].astype(BF16), wi_t[...]).astype(BF16).astype(F32)
        hg[tokens, :] = hidden_grad
        normed_grad = hidden_grad * gain
        mine = normed[tokens]
        along = jnp.mean(normed_grad * mine, axis=-1, keepdims=True)
        inner = normed_grad - jnp.mean(normed_grad, axis=-1, keepdims=True) - mine * along
        input_grad = grad + inverse[tokens] * inner
        gsend[z] = jnp.concatenate([input_grad, jnp.zeros((8, C), F32)], axis=0).astype(BF16)

        @pl.when(jnp.logical_not(first))
        def _(z=z):
            downs[z].start()

        for b in range(GROUPS):
            wide[b, pl.ds(1 - z, TOK, stride=LEVELS), :] = input_grad[:, b * LANES:(b + 1) * LANES]

    wide_share = ms.shape[2]
    gain_grad = jnp.sum(hg[...] * normed, axis=0, keepdims=True)
    spare = round_up(C, wide_share) - C
    if spare:
        gain_grad = jnp.concatenate([gain_grad, jnp.zeros((1, spare), F32)], axis=1)
    gain_parts = [gain_grad[:, at:at + wide_share] for at in range(0, C, wide_share)]
    gain_rows = jnp.concatenate(gain_parts + [jnp.zeros((16 - len(gain_parts), wide_share), F32)], axis=0).astype(BF16)
    for i in range(na):
        ms[i, 0:WIN, :] = pg[:, i * e1:(i + 1) * e1 - rest].astype(BF16)
        ms[i, WIN:WIN + 16, :] = gain_rows
    share_of_grad = share_copies(ms, mr, msend_sem, mrecv_sem)
    for copy in share_of_grad:
        copy.start()
    tails = [pg[:, (i + 1) * e1 - rest:(i + 1) * e1] for i in range(na)]
    tails = jnp.concatenate(tails, axis=1).T
    tails = jnp.concatenate([tails, jnp.zeros((na * rest, 2 * LANES - WIN), F32)], axis=1).astype(BF16)
    for i in range(na):
        ts[i] = tails[i * rest:(i + 1) * rest]
    tail_of_grad = share_copies(ts, tr, tsend_sem, trecv_sem)
    for copy in tail_of_grad:
        copy.start()
    pl.when(sec >= ns // 2)(send_exits)

    for i, (a, l) in enumerate(quarters):
        for r in range(3):
            row = ((3 * a + r) * WLON + 6 * l) * LEVELS
            for b in range(GROUPS):
                part = wide[b, row:row + 6 * LEVELS, :].reshape(6, LEVELS, LANES)
                rb[i, r, :, :, b * LANES:(b + 1) * LANES] = part.astype(BF16)
    home = pltpu.make_async_copy(rb.at[0], quarter(ig_out, 0), load_sem.at[8])
    home.start()
    back_copies = [
        pltpu.make_async_remote_copy(
            src_ref=rb.at[i], dst_ref=quarter(ig_out, i), send_sem=bksend_sem.at[i], recv_sem=bkrecv_sem.at[i],
            device_id=towards(i, 1), device_id_type=MESH,
        )
        for i in (3, 2, 1)
    ]
    for copy in back_copies:
        copy.start()

    folded = jnp.zeros((PAIRS, 2 * LANES), F32)
    for lq in range(WLON):
        part = ds[pl.ds(lq, PAIRS, stride=WLON), :].astype(BF16)
        folded += dot_t(part, s_v[:, lq * LANES:(lq + 1) * LANES])
    t0[...] = folded[:, :LANES]
    t1[...] = folded[:, LANES:]
    for u in range(8):
        upper, lower = (
            jnp.concatenate([t0[rows, :], t1[rows, :]], axis=1)
            for rows in (pl.ds(u // 4 * HEADS * WLAT + BIAS_ROWS[u % 4] + k, HEADS, stride=WLAT) for k in range(2))
        )
        half = width // 2
        if u % 2 == 0:
            lower = lower[:, :half]
        else:
            upper, lower = upper[:, half:width], lower[:, :width]
        both = jnp.concatenate([upper[:, :width], lower, jnp.zeros((HEADS, 2 * LANES - RELPOS // 16), F32)], axis=1)
        bsb[u] = jnp.concatenate([both, jnp.zeros((16 - HEADS, 2 * LANES), F32)], axis=0).astype(BF16)
    if no == 16:
        def bias_copy(u, k):
            target = u if u < 4 else u + 8
            return target, pltpu.make_async_remote_copy(
                src_ref=bsb.at[u], dst_ref=brb.at[k], send_sem=bsend_sem.at[u], recv_sem=brecv_sem.at[k],
                device_id={n_lon: jnp.int32(target)}, device_id_type=MESH,
            )

        for u in range(8):
            target, copy = bias_copy(u, lon)

            @pl.when(lon != target)
            def _(copy=copy):
                copy.start()

    loads[6].wait()
    own = ms[lat]
    entry = t_dot(own[:WIN], hidden)
    entry_tail = dot(ts[lat][:, :WIN], hidden)
    exits = es[lat].astype(F32)
    gain_total = own[WIN:WIN + 16].astype(F32)
    for i in reversed(range(len(steps))):
        k = slot(steps[i])
        if steps[i] != (0, 1):
            hidden_copies[i].wait_recv()
        for copies in (exit_copies, share_of_grad, tail_of_grad):
            copies[i].wait_recv()
        entry += t_dot(mr[k][:WIN], hr[k])
        entry_tail += dot(tr[k][:, :WIN], hr[k])
        exits += er[k].astype(F32)
        gain_total += mr[k][WIN:WIN + 16].astype(F32)
    gain_total = jnp.concatenate([gain_total[i:i + 1] for i in range(len(gain_parts))], axis=1)[:, :C]
    total = jnp.concatenate([entry, entry_tail, exits, gain_total, jnp.zeros((15, C), F32)], axis=0)
    sb2[...] = dot(p2_v[...], total.astype(BF16)).astype(BF16).reshape(sb2.shape)
    second_copies = [
        pltpu.make_async_remote_copy(
            src_ref=sb2.at[at_lon(k)], dst_ref=rb2.at[k], send_sem=s2send.at[k], recv_sem=s2recv.at[k],
            device_id={n_lon: at_lon(k)}, device_id_type=MESH,
        )
        for k in turns
    ]
    for copy in second_copies:
        copy.start()

    if no == 16:
        keeps = jnp.logical_or(lon < 4, lon >= 12)
        bias_out[...] = jnp.zeros_like(bias_out)

        @pl.when(keeps)
        def _():
            for s in range(no):
                @pl.when(lon != s)
                def _():
                    bias_copy(0, s)[1].wait_recv()
            brb[lon] = bsb[jnp.where(lon < 4, lon, lon - 8)]
            total = brb[0].astype(F32)
            for s in range(1, no):
                total += brb[s].astype(F32)
            bias_out[...] = total[:HEADS, :RELPOS // 16]

        for u in range(8):
            target, copy = bias_copy(u, lon)

            @pl.when(lon != target)
            def _(copy=copy):
                copy.wait_send()
    else:
        bias_out[...] = jnp.zeros_like(bias_out)

    e2, x2 = e1 // no, x1 // no
    for copy in second_copies:
        copy.wait_recv()
    total = sb2[lon].astype(F32)
    for k in range(1, no):
        total += rb2[k].astype(F32)
    sums_out[...] = total
    gain_row = jnp.broadcast_to(total[e2 + x2:e2 + x2 + 1], (8, C))
    gain_out[...] = pltpu.roll(gain_row, lax.rem(C - (lat * no + lon) * x2, C), 1)

    home.wait()
    for copy in back_copies:
        copy.wait_recv()
    for copy in x_copies + back_copies + hidden_copies + exit_copies + share_of_grad + tail_of_grad + second_copies:
        copy.wait_send()

    @pl.when(last)
    def _():
        for copy in c_copies:
            copy.wait_send()

    @pl.when(jnp.logical_not(first))
    def _():
        for copy in downs:
            copy.wait_send()


def call_kernel(sizes, names, args):
    ns, na, no = sizes
    e1, x1 = 3 * C // na, C // na
    e2, x2 = e1 // no, x1 // no
    r2 = round_up(e2 + x2 + 1, 16)
    spread = jnp.asarray(spread_table(), BF16)
    shares = jnp.asarray(share_table(e1, x1, 16, no, r2), BF16)
    hbm = pl.BlockSpec(memory_space=pltpu.HBM)
    vmem = pl.BlockSpec(memory_space=pltpu.VMEM)
    dma = pltpu.SemaphoreType.DMA
    n = LEVELS * GROUPS
    tile = (WLAT, WLON, LEVELS, C)
    parts = (4, WLAT // 2, WLON // 2, LEVELS, C)
    return pl.pallas_call(
        functools.partial(kernel, sizes, names),
        out_shape=(
            jax.ShapeDtypeStruct(tile, BF16),
            jax.ShapeDtypeStruct((r2, C), F32),
            jax.ShapeDtypeStruct((8, C), F32),
            jax.ShapeDtypeStruct((HEADS, RELPOS // 16), F32),
        ),
        in_specs=[hbm] * 8,
        out_specs=(hbm, vmem, vmem, vmem),
        scratch_shapes=[
            pltpu.VMEM(parts, BF16),
            pltpu.VMEM(parts, BF16),
            pltpu.VMEM((C, 3 * C), BF16),
            pltpu.VMEM((C, C), BF16),
            pltpu.VMEM((3 * C, C), BF16),
            pltpu.VMEM((C, C), BF16),
            pltpu.VMEM((1, C), F32),
            pltpu.VMEM((HEADS, 1, RELPOS), F32),
            pltpu.VMEM(spread.shape, BF16),
            pltpu.VMEM(shares.shape, BF16),
            pltpu.VMEM((PAIRS, LANES), F32),
            pltpu.VMEM((PAIRS, LANES), F32),
            pltpu.VMEM((ROWS, LANES), F32),
            pltpu.VMEM((GROUPS, WIN, LANES), F32),
            pltpu.VMEM((WIN, C), F32),
            pltpu.VMEM((WIN, C), F32),
            pltpu.VMEM((ROWS, LANES), F32),
            pltpu.VMEM((n, LANES, STACK), BF16),
            pltpu.VMEM((n, STACK, LANES), BF16),
            pltpu.VMEM((n, LANES, LANES), BF16),
            pltpu.VMEM((n, 2 * LANES, LANES), BF16),
            pltpu.VMEM((ROWS, LANES), F32),
            pltpu.VMEM((WIN, C), F32),
            pltpu.VMEM((ROWS, LANES), F32),
            pltpu.VMEM((WIN, 3 * C), F32),
            pltpu.VMEM((WIN, C), F32),
            pltpu.VMEM((LEVELS, TOK + 8, C), BF16),
            pltpu.VMEM((LEVELS, TOK + 8, C), BF16),
            pltpu.VMEM(parts, BF16),
            pltpu.VMEM((WIN, C), BF16),
            pltpu.VMEM((na, WIN, C), BF16),
            pltpu.VMEM((na, x1, C), BF16),
            pltpu.VMEM((na, x1, C), BF16),
            pltpu.VMEM((na, WIN + 16, e1 - e1 % LANES), BF16),
            pltpu.VMEM((na, WIN + 16, e1 - e1 % LANES), BF16),
            pltpu.VMEM((na, e1 % LANES, 2 * LANES), BF16),
            pltpu.VMEM((na, e1 % LANES, 2 * LANES), BF16),
            pltpu.VMEM((no, r2, C), BF16),
            pltpu.VMEM((no, r2, C), BF16),
            pltpu.VMEM((8, 16, 2 * LANES), BF16),
            pltpu.VMEM((16, 16, 2 * LANES), BF16),
            dma((9,)), dma((4,)), dma((4,)), dma((4,)), dma((4,)), dma((2,)), dma((2,)), dma((4,)), dma((4,)),
            dma((na,)), dma((na,)), dma((na,)), dma((na,)), dma((na,)), dma((na,)), dma((na,)), dma((na,)), dma((no,)), dma((no,)), dma((8,)), dma((16,)),
        ],
        compiler_params=pltpu.CompilerParams(collective_id=0, has_side_effects=True, vmem_limit_bytes=56 * 2**20),
    )(*args, spread, shares)


def finish(share, ig_in, sums_in, gain_in, bias_in, ig_out, entry_out, exit_out, gain_out, bias_out):
    ig_out[...] = ig_in[...]
    entry_out[:, 0, :] = sums_in[0:3 * share]
    exit_out[:, 0, :] = sums_in[3 * share:4 * share]
    gain_out[...] = gain_in[0:1, 0:share]
    bias_out[:, 0, :] = bias_in[...]


def call_finish(share, *results):
    vmem = pl.BlockSpec(memory_space=pltpu.VMEM)
    return pl.pallas_call(
        functools.partial(finish, share),
        out_shape=(
            jax.ShapeDtypeStruct(results[0].shape, BF16),
            jax.ShapeDtypeStruct((3 * share, 1, C), F32),
            jax.ShapeDtypeStruct((share, 1, C), F32),
            jax.ShapeDtypeStruct((1, share), F32),
            jax.ShapeDtypeStruct((HEADS, 1, RELPOS // 16), F32),
        ),
        in_specs=[vmem] * 4,
        out_specs=(vmem,) * 5,
    )(*results)


def per_device(sizes, names, block_inputs, cotangent, input_projection, output_projection, norm_gain, earth_bias):
    ns, na, no = sizes
    args = (
        block_inputs[0].transpose(1, 2, 0, 3), cotangent.transpose(1, 2, 0, 3), input_projection, output_projection,
        norm_gain, earth_bias[0, 0, 0][:, None],
    )
    input_grad, sums, gain, bias = call_kernel(sizes, names, args)
    input_grad, entry, exits, gain, bias = call_finish(C // (na * no), input_grad, sums, gain, bias)
    return (
        input_grad.transpose(2, 0, 1, 3)[None], entry.transpose(1, 2, 0), exits.transpose(1, 2, 0), gain,
        bias[None, None].transpose(0, 1, 3, 2, 4),
    )


def solution(mesh):
    names = ("section", "lat", "lon")
    sizes = tuple(mesh.shape[name] for name in names)
    in_specs = (
        P("section", None, "lat", "lon", None),
        P(None, "lat", "lon", None),
        P("section", None, None),
        P("section", None, None),
        P("section", None),
        P("section", None, "lat", None, None),
    )
    out_specs = (
        P("section", None, "lat", "lon", None),
        P("section", None, ("lat", "lon")),
        P("section", None, ("lat", "lon")),
        P("section", ("lat", "lon")),
        P("section", None, "lat", None, "lon"),
    )
    return jax.shard_map(
        functools.partial(per_device, sizes, names), mesh=mesh, in_specs=in_specs, out_specs=out_specs, check_vma=False
    )
```
